32 devices in a mesh: dp: 4 (over z), seq: 8 (over y, x, core).
Axes of the slice: x: 2, y: 2, z: 4, core: 2. Of those that a mesh axis runs over, the one named last changes fastest.
Arguments:
- values: bfloat16 [4, 65536, 512], P('dp', 'seq'), may hold values from -6 to 6
- cotangent: bfloat16 [4, 65536, 512], P('dp', 'seq'), may hold values from -6 to 6
- kernel: bfloat16 [65536, 512], P('seq'), may hold values from -6 to 6
- left_factor: bfloat16 [256, 256, 256], P('seq'), may hold values from -0.375 to 0.375
- right_factor: bfloat16 [256, 256, 256], P('seq'), may hold values from -0.375 to 0.375
Outputs:
- mixed: bfloat16 [4, 65536, 512], P('dp', 'seq')
- values_grad: bfloat16 [4, 65536, 512], P('dp', 'seq')
- kernel_grad: float32 [65536, 512], P(('seq', 'dp'))
The draws below stay inside these ranges and needn't reach their ends.
All inputs are finite; a program needn't handle non-finite values.
Results may differ from the reference program's by a relative error of at most 0.018.
Values may be sent and summed in bfloat16 or wider, within the bound.
No kernel may reach another device: no remote copies, remote signals or barrier semaphores. Data moves between devices by JAX's collectives and lax.ppermute only.
A program may use at most 192 MiB of HBM per device.

```python
import jax
import jax.numpy as jnp
from jax import lax

NB = 256
C = 512
L = 65536
SEQS = 4


def shard_levels(stream_key, dims, pieces, least, largest):
    level = 1.0
    for axis_at, shards_of in pieces:
        heights = jax.random.uniform(jax.random.fold_in(jax.random.fold_in(stream_key, 6), axis_at), (shards_of,), jnp.float32, least / len(pieces), largest / len(pieces))
        level = level * jnp.repeat(jnp.exp(heights), dims[axis_at] // shards_of).reshape((-1,) + (1,) * (len(dims) - 1 - axis_at))
    return level


def gaussian(key, dims, width, limit, pieces=(), dtype=jnp.bfloat16):
    loudness = shard_levels(key, dims, pieces, -0.22, 0.18) if pieces else 1.0
    drawn = jax.random.normal(key, dims, jnp.float32) * width * loudness
    return jnp.minimum(jnp.maximum(drawn, -limit), limit).astype(dtype)


def setup_inputs(seed: int = 0) -> dict:
    splits = jax.random.split(jax.random.key(seed), 6)
    return {
        "values": gaussian(splits[0], (SEQS, L, C), 1.0, 6.0, ((0, 4), (1, 8))),
        "cotangent": gaussian(splits[1], (SEQS, L, C), 1.0, 6.0, ((0, 4), (1, 8))),
        "kernel": gaussian(splits[2], (L, C), 1.0, 6.0, ((0, 8),)),
        "left_factor": gaussian(splits[3], (NB, NB, NB), NB ** -0.5, 0.375, ((0, 8),)),
        "right_factor": gaussian(splits[4], (NB, NB, NB), NB ** -0.5, 0.375, ((0, 8),)),
    }


def forward_transform(field, left_factor, right_factor):
    blocks_view = field.astype(jnp.float32).reshape(NB, NB, C)
    first = jnp.einsum('ikj,ijc->ikc', left_factor.astype(jnp.float32), blocks_view).astype(jnp.bfloat16)
    result = jnp.einsum('kli,ikc->klc', right_factor.astype(jnp.float32), first.astype(jnp.float32))
    return result.reshape(NB * NB, C)


def transpose_transform(field, left_factor, right_factor):
    blocks_view = field.astype(jnp.float32).reshape(NB, NB, C)
    back = jnp.einsum('kli,klc->ikc', right_factor.astype(jnp.float32), blocks_view).astype(jnp.bfloat16)
    result = jnp.einsum('ikj,ikc->ijc', left_factor.astype(jnp.float32), back.astype(jnp.float32))
    return result.reshape(NB * NB, C)


def reference(values, cotangent, kernel, left_factor, right_factor):
    kernel_wide = kernel.astype(jnp.float32)

    def one_sequence(total, inputs):
        source, upstream = inputs
        spectrum = forward_transform(source, left_factor, right_factor).astype(jnp.bfloat16)
        filtered = (kernel_wide * spectrum.astype(jnp.float32)).astype(jnp.bfloat16)
        convolved = transpose_transform(filtered, left_factor, right_factor)
        mixed = (source.astype(jnp.float32) * convolved).astype(jnp.bfloat16)
        gated_grad = (upstream.astype(jnp.float32) * source.astype(jnp.float32)).astype(jnp.bfloat16)
        spectrum_grad = forward_transform(gated_grad, left_factor, right_factor)
        total = total + spectrum_grad * spectrum.astype(jnp.float32)
        weighted_grad = (kernel_wide * spectrum_grad).astype(jnp.bfloat16)
        carried = transpose_transform(weighted_grad, left_factor, right_factor)
        values_grad = (upstream.astype(jnp.float32) * convolved + carried).astype(jnp.bfloat16)
        return total, (mixed, values_grad)

    start_total = jnp.zeros((NB * NB, C), jnp.float32)
    kernel_grad, outputs = lax.scan(one_sequence, start_total, (values, cotangent))
    return outputs[0], outputs[1], kernel_grad
```

```python
import jax
import jax.numpy as jnp
from jax import lax
from jax.sharding import PartitionSpec as P

CHUNKS = 4


def per_device(values, cotangent, kernel, left_factor, right_factor):
    sequences, row_count, channels = values.shape
    local_blocks, order, _ = left_factor.shape
    ranks = order // local_blocks
    width = channels // CHUNKS

    def exchange(spread):
        return lax.all_to_all(spread, "seq", split_axis=0, concat_axis=0, tiled=True)

    def rounded(x):
        return x.astype(jnp.bfloat16)

    received = []
    sources = []
    for q in range(CHUNKS):
        part = slice(q * width, (q + 1) * width)
        source = values[..., part].reshape(sequences, local_blocks, order, width)
        upstream = cotangent[..., part].reshape(sequences, local_blocks, order, width)
        sources.append((source, upstream))
        gated = rounded(source.astype(jnp.float32) * upstream.astype(jnp.float32))
        both = jnp.concatenate([source, gated], axis=0)
        first = rounded(
            jnp.einsum("ikj,sijc->sikc", left_factor, both, preferred_element_type=jnp.float32)
        )
        first = first.reshape(2 * sequences, local_blocks, ranks, local_blocks, width)
        received.append(exchange(first.transpose(2, 0, 1, 3, 4)))

    returned = []
    grads = []
    for q in range(CHUNKS):
        part = slice(q * width, (q + 1) * width)
        kernel_wide = kernel[:, part].astype(jnp.float32).reshape(1, local_blocks, order, width)
        portion = received[q].transpose(1, 0, 2, 3, 4).reshape(2 * sequences, order, local_blocks, width)
        result = jnp.einsum(
            "kli,sikc->sklc", right_factor, portion, preferred_element_type=jnp.float32
        )
        spectrum = rounded(result[:sequences])
        spectrum_grad = result[sequences:]
        spectrum_wide = spectrum.astype(jnp.float32)
        filtered = rounded(kernel_wide * spectrum_wide)
        weighted = rounded(kernel_wide * spectrum_grad)
        term = jnp.sum(spectrum_grad * spectrum_wide, axis=0).reshape(row_count, width)
        grads.append(
            lax.psum_scatter(rounded(term), "dp", scatter_dimension=0, tiled=True)
        )
        back = rounded(
            jnp.einsum(
                "kli,sklc->sikc",
                right_factor,
                jnp.concatenate([filtered, weighted], axis=0),
                preferred_element_type=jnp.float32,
            )
        )
        back = back.reshape(2 * sequences, ranks, local_blocks, local_blocks, width)
        returned.append(exchange(back.transpose(1, 0, 2, 3, 4)))

    mixed = []
    values_grad = []
    for q in range(CHUNKS):
        source, upstream = sources[q]
        portion = returned[q].transpose(1, 2, 0, 3, 4).reshape(2 * sequences, local_blocks, order, width)
        result = jnp.einsum(
            "ikj,sikc->sijc", left_factor, portion, preferred_element_type=jnp.float32
        )
        convolved = result[:sequences]
        carried = result[sequences:]
        mixed.append(rounded(source.astype(jnp.float32) * convolved))
        values_grad.append(rounded(upstream.astype(jnp.float32) * convolved + carried))

    def whole(parts):
        return jnp.concatenate(parts, axis=-1).reshape(sequences, row_count, channels)

    return whole(mixed), whole(values_grad), jnp.concatenate(grads, axis=-1).astype(jnp.float32)


def solution(mesh):
    in_specs = (
        P("dp", "seq", None),
        P("dp", "seq", None),
        P("seq", None),
        P("seq", None, None),
        P("seq", None, None),
    )
    out_specs = (P("dp", "seq", None), P("dp", "seq", None), P(("seq", "dp"), None))
    return jax.shard_map(
        per_device, mesh=mesh, in_specs=in_specs, out_specs=out_specs, check_vma=False
    )
```

```python
import functools

import jax
import jax.numpy as jnp
from jax import lax
from jax.experimental import pallas as pl
from jax.experimental.pallas import tpu as pltpu
from jax.sharding import PartitionSpec as P

WIDTH = 128
ROWS = 16
VMEM_LIMIT = 48 * 1024 * 1024


def left_forward_kernel(rank_ref, values_ref, cotangent_ref, left_ref, *sends):
    ranks = len(sends)
    blocks, order, _ = left_ref.shape
    share = order // ranks
    rank = rank_ref[0]
    for i in range(blocks):
        rows = slice(i * order, (i + 1) * order)
        source = values_ref[0, rows, :]
        gated = source.astype(jnp.float32) * cotangent_ref[0, rows, :].astype(jnp.float32)
        both = jnp.concatenate([source, gated.astype(jnp.bfloat16)], axis=1)
        factor = jnp.concatenate(
            [left_ref[i, pl.ds(pl.multiple_of((rank ^ m) * share, share), share), :] for m in range(ranks)],
            axis=0,
        )
        first = jnp.dot(factor, both, preferred_element_type=jnp.float32).astype(jnp.bfloat16)
        for m in range(ranks):
            sends[m][i] = first[m * share : (m + 1) * share]


def right_kernel(rank_ref, kernel_ref, right_ref, *refs):
    ranks = (len(refs) - 3) // 2
    arrived, sends = refs[:ranks], refs[ranks : 2 * ranks]
    term_ref, gathered, scattered = refs[2 * ranks :]
    share, rows, lanes = arrived[0].shape
    order = right_ref.shape[1]
    width = lanes // 2
    rank = rank_ref[0]
    halves = [slice(0, width), slice(width, lanes)]

    def span(m):
        return pl.ds(pl.multiple_of((rank ^ m) * (share * rows), share * rows), share * rows)

    for m in range(ranks):
        for half in range(2):
            block = arrived[m][:, :, halves[half]].astype(jnp.float32)
            gathered[half, span(m), :] = block.reshape(share * rows, width)

    def step(k, carry):
        both = jnp.concatenate(
            [gathered[half, pl.ds(k, order, stride=rows), :] for half in range(2)], axis=1
        ).astype(jnp.bfloat16)
        factor = right_ref[k]
        result = jnp.dot(factor, both, preferred_element_type=jnp.float32)
        spectrum = result[:, :width].astype(jnp.bfloat16).astype(jnp.float32)
        spectrum_grad = result[:, width:]
        here = pl.ds(pl.multiple_of(k * order, order), order)
        kernel_wide = kernel_ref[here, :].astype(jnp.float32)
        term_ref[here, :] = (spectrum_grad * spectrum).astype(jnp.bfloat16)
        domain = jnp.concatenate(
            [
                (kernel_wide * spectrum).astype(jnp.bfloat16),
                (kernel_wide * spectrum_grad).astype(jnp.bfloat16),
            ],
            axis=1,
        )
        back = lax.dot_general(
            factor, domain, (((0,), (0,)), ((), ())), preferred_element_type=jnp.float32
        )
        for half in range(2):
            scattered[half, pl.ds(k, order, stride=rows), :] = back[:, halves[half]]
        return carry

    lax.fori_loop(0, rows, step, 0)

    for m in range(ranks):
        for half in range(2):
            block = scattered[half, span(m), :].astype(jnp.bfloat16)
            sends[m][:, :, halves[half]] = block.reshape(share, rows, width)


def left_back_kernel(ranks, rank_ref, values_ref, cotangent_ref, left_ref, reduced_ref, *refs):
    arrived = refs[:ranks]
    mixed_ref, values_grad_ref, kernel_grad_ref = refs[-3:]
    blocks, order, _ = left_ref.shape
    share = order // ranks
    width = values_ref.shape[2]
    rank = rank_ref[0]
    for i in range(blocks):
        rows = slice(i * order, (i + 1) * order)
        factor = jnp.concatenate(
            [left_ref[i, pl.ds(pl.multiple_of((rank ^ m) * share, share), share), :] for m in range(ranks)],
            axis=0,
        )
        back = jnp.concatenate([arrived[m][i] for m in range(ranks)], axis=0)
        result = lax.dot_general(
            factor, back, (((0,), (0,)), ((), ())), preferred_element_type=jnp.float32
        )
        convolved, carried = result[:, :width], result[:, width:]
        source = values_ref[0, rows, :].astype(jnp.float32)
        upstream = cotangent_ref[0, rows, :].astype(jnp.float32)
        mixed_ref[0, rows, :] = (source * convolved).astype(jnp.bfloat16)
        values_grad_ref[0, rows, :] = (upstream * convolved + carried).astype(jnp.bfloat16)
    kernel_grad_ref[...] = reduced_ref[...].astype(jnp.float32)


def per_device(values, cotangent, kernel, left_factor, right_factor, ranks, groups):
    sequences, row_count, channels = values.shape
    local, order, _ = left_factor.shape
    width = WIDTH
    lanes = 2 * width
    blocks = min(4, local)
    rows = min(ROWS, local)
    chunks = channels // width
    rank = lax.axis_index("seq").astype(jnp.int32).reshape(1)
    params = pltpu.CompilerParams(vmem_limit_bytes=VMEM_LIMIT)
    buffer = jax.ShapeDtypeStruct((local, local, lanes), jnp.bfloat16)

    def field_spec(q):
        return pl.BlockSpec((1, blocks * order, width), lambda g, rank: (0, g, q))

    def factor_spec(size):
        return pl.BlockSpec((size, order, order), lambda g, rank: (g, 0, 0))

    def left_forward(q):
        return pl.pallas_call(
            left_forward_kernel,
            out_shape=[buffer] * ranks,
            grid_spec=pltpu.PrefetchScalarGridSpec(
                num_scalar_prefetch=1,
                grid=(local // blocks,),
                in_specs=[field_spec(q), field_spec(q), factor_spec(blocks)],
                out_specs=[pl.BlockSpec((blocks, local, lanes), lambda g, rank: (g, 0, 0))] * ranks,
            ),
            compiler_params=params,
            cost_estimate=pl.CostEstimate(
                flops=2 * local * order * order * lanes,
                bytes_accessed=12 * 1024 * 1024,
                transcendentals=0,
            ),
        )(rank, values, cotangent, left_factor)

    def exchange(sends):
        arrived = [sends[0]]
        for m in range(1, ranks):
            arrived.append(lax.ppermute(sends[m], "seq", [(r, r ^ m) for r in range(ranks)]))
        return arrived

    def right_both(q, arrived):
        moved = pl.BlockSpec((local, rows, lanes), lambda g, rank: (0, g, 0))
        return pl.pallas_call(
            right_kernel,
            out_shape=[buffer] * ranks + [jax.ShapeDtypeStruct((row_count, width), jnp.bfloat16)],
            grid_spec=pltpu.PrefetchScalarGridSpec(
                num_scalar_prefetch=1,
                grid=(local // rows,),
                in_specs=[
                    pl.BlockSpec((rows * order, width), lambda g, rank: (g, q)),
                    factor_spec(rows),
                ]
                + [moved] * ranks,
                out_specs=[moved] * ranks
                + [pl.BlockSpec((rows * order, width), lambda g, rank: (g, 0))],
                scratch_shapes=[
                    pltpu.VMEM((2, order * rows, width), jnp.float32),
                    pltpu.VMEM((2, order * rows, width), jnp.float32),
                ],
            ),
            compiler_params=params,
            cost_estimate=pl.CostEstimate(
                flops=4 * local * order * order * lanes,
                bytes_accessed=16 * 1024 * 1024,
                transcendentals=0,
            ),
        )(rank, kernel, right_factor, *arrived)

    def left_back(q, arrived, reduced, outputs):
        steps = local // blocks
        shard = row_count // groups
        out_shape = [
            jax.ShapeDtypeStruct(values.shape, jnp.bfloat16),
            jax.ShapeDtypeStruct(values.shape, jnp.bfloat16),
            jax.ShapeDtypeStruct((shard, channels), jnp.float32),
        ]
        earlier = list(outputs) if outputs else []
        aliases = {5 + ranks + n: n for n in range(len(earlier))}
        return pl.pallas_call(
            functools.partial(left_back_kernel, ranks),
            out_shape=out_shape,
            grid_spec=pltpu.PrefetchScalarGridSpec(
                num_scalar_prefetch=1,
                grid=(steps,),
                in_specs=[
                    field_spec(q),
                    field_spec(q),
                    factor_spec(blocks),
                    pl.BlockSpec((shard // steps, width), lambda g, rank: (g, 0)),
                ]
                + [pl.BlockSpec((blocks, local, lanes), lambda g, rank: (g, 0, 0))] * ranks
                + [pl.BlockSpec(memory_space=pl.ANY)] * len(earlier),
                out_specs=[
                    field_spec(q),
                    field_spec(q),
                    pl.BlockSpec((shard // steps, width), lambda g, rank: (g, q)),
                ],
            ),
            input_output_aliases=aliases,
            compiler_params=params,
            cost_estimate=pl.CostEstimate(
                flops=2 * local * order * order * lanes,
                bytes_accessed=16 * 1024 * 1024,
                transcendentals=0,
            ),
        )(rank, values, cotangent, left_factor, reduced, *arrived, *earlier)

    received = [exchange(left_forward(q)) for q in range(chunks)]
    returned, reduced = [], []
    for q in range(chunks):
        *sends, term = right_both(q, received[q])
        returned.append(exchange(sends))
        reduced.append(lax.psum_scatter(term, "dp", scatter_dimension=0, tiled=True))
    outputs = None
    for q in range(chunks):
        outputs = left_back(q, returned[q], reduced[q], outputs)
    return tuple(outputs)


def solution(mesh):
    in_specs = (
        P("dp", "seq", None),
        P("dp", "seq", None),
        P("seq", None),
        P("seq", None, None),
        P("seq", None, None),
    )
    out_specs = (P("dp", "seq", None), P("dp", "seq", None), P(("seq", "dp"), None))
    return jax.shard_map(
        functools.partial(per_device, ranks=mesh.shape["seq"], groups=mesh.shape["dp"]),
        mesh=mesh,
        in_specs=in_specs,
        out_specs=out_specs,
        check_vma=False,
    )
```

```python
import functools

import jax
import jax.numpy as jnp
from jax import lax
from jax.experimental import pallas as pl
from jax.experimental.pallas import tpu as pltpu
from jax.sharding import PartitionSpec as P

WIDTH = 128
ROWS = 16
VMEM_LIMIT = 60 * 1024 * 1024
COST = pl.CostEstimate(flops=1024, bytes_accessed=1024, transcendentals=0)
SHARED = 4
EARLY = 2
UNROLL = 4
TOKEN = (8, 128)


def moves_of(ranks):
    return [0] + list(range(2, ranks, 2)) + list(range(3, ranks, 2)) + [1]


def left_forward_kernel(ranks, rank_ref, values_ref, cotangent_ref, left_ref, *refs):
    moves = moves_of(ranks)
    *sends, token_ref = refs[-ranks - 1 :]
    token_ref[...] = jnp.zeros_like(token_ref)
    blocks, order, _ = left_ref.shape
    share = order // ranks
    rank = rank_ref[0]
    for i in range(blocks):
        rows = slice(i * order, (i + 1) * order)
        source = values_ref[0, rows, :]
        gated = source.astype(jnp.float32) * cotangent_ref[0, rows, :].astype(jnp.float32)
        both = jnp.concatenate([source, gated.astype(jnp.bfloat16)], axis=1)
        factor = jnp.concatenate(
            [left_ref[i, pl.ds(pl.multiple_of((rank ^ m) * share, share), share), :] for m in moves],
            axis=0,
        )
        first = jnp.dot(factor, both, preferred_element_type=jnp.float32).astype(jnp.bfloat16)
        for m in range(ranks):
            sends[m][i] = first[m * share : (m + 1) * share]


def right_kernel(ranks, rank_ref, kernel_ref, right_ref, *refs):
    arrived = refs[:ranks]
    *sends, term_ref, token_ref, gathered, scattered = refs[-ranks - 4 :]
    token_ref[...] = jnp.zeros_like(token_ref)
    share, rows, lanes = arrived[0].shape
    order = right_ref.shape[1]
    width = lanes // 2
    rank = rank_ref[0]
    halves = [slice(0, width), slice(width, lanes)]

    moves = moves_of(ranks)

    def span(n):
        m = moves[n]
        return pl.ds(pl.multiple_of((rank ^ m) * (share * rows), share * rows), share * rows)

    for m in range(ranks):
        for half in range(2):
            block = arrived[m][:, :, halves[half]].astype(jnp.float32)
            gathered[half, span(m), :] = block.reshape(share * rows, width)

    def step(k, carry):
        both = jnp.concatenate(
            [gathered[half, pl.ds(k, order, stride=rows), :] for half in range(2)], axis=1
        ).astype(jnp.bfloat16)
        factor = right_ref[k]
        result = jnp.dot(factor, both, preferred_element_type=jnp.float32)
        spectrum = result[:, :width].astype(jnp.bfloat16).astype(jnp.float32)
        spectrum_grad = result[:, width:]
        here = pl.ds(pl.multiple_of(k * order, order), order)
        kernel_wide = kernel_ref[here, :].astype(jnp.float32)
        term_ref[here, :] = (spectrum_grad * spectrum).astype(jnp.bfloat16)
        domain = jnp.concatenate(
            [
                (kernel_wide * spectrum).astype(jnp.bfloat16),
                (kernel_wide * spectrum_grad).astype(jnp.bfloat16),
            ],
            axis=1,
        )
        back = lax.dot_general(
            factor, domain, (((0,), (0,)), ((), ())), preferred_element_type=jnp.float32
        )
        for half in range(2):
            scattered[half, pl.ds(k, order, stride=rows), :] = back[:, halves[half]]
        return carry

    def several(g, carry):
        for n in range(UNROLL):
            step(g * UNROLL + n, carry)
        return carry

    lax.fori_loop(0, rows // UNROLL, several, 0)

    for m in range(ranks):
        for half in range(2):
            block = scattered[half, span(m), :].astype(jnp.bfloat16)
            sends[m][:, :, halves[half]] = block.reshape(share, rows, width)


def left_back_kernel(ranks, terms, rank_ref, values_ref, cotangent_ref, left_ref, *refs):
    moves = moves_of(ranks)
    arrived, reduced = refs[:ranks], refs[ranks : ranks + terms]
    mixed_ref, values_grad_ref, kernel_grad_ref, token_ref = refs[-4:]
    token_ref[...] = jnp.zeros_like(token_ref)
    blocks, order, _ = left_ref.shape
    share = order // ranks
    width = values_ref.shape[2]
    rank = rank_ref[0]
    for i in range(blocks):
        rows = slice(i * order, (i + 1) * order)
        factor = jnp.concatenate(
            [left_ref[i, pl.ds(pl.multiple_of((rank ^ m) * share, share), share), :] for m in moves],
            axis=0,
        )
        back = jnp.concatenate([arrived[m][i] for m in range(ranks)], axis=0)
        result = lax.dot_general(
            factor, back, (((0,), (0,)), ((), ())), preferred_element_type=jnp.float32
        )
        convolved, carried = result[:, :width], result[:, width:]
        source = values_ref[0, rows, :].astype(jnp.float32)
        upstream = cotangent_ref[0, rows, :].astype(jnp.float32)
        mixed_ref[0, rows, :] = (source * convolved).astype(jnp.bfloat16)
        values_grad_ref[0, rows, :] = (upstream * convolved + carried).astype(jnp.bfloat16)
    for n in range(terms):
        lanes = reduced[n].shape[1]
        kernel_grad_ref[:, n * lanes : (n + 1) * lanes] = reduced[n][...].astype(jnp.float32)


def per_device(values, cotangent, kernel, left_factor, right_factor, ranks, groups):
    sequences, row_count, channels = values.shape
    local, order, _ = left_factor.shape
    width = WIDTH
    lanes = 2 * width
    blocks = min(4, local)
    rows = min(ROWS, local)
    chunks = channels // width
    moves = moves_of(ranks)
    rank = lax.axis_index("seq").astype(jnp.int32).reshape(1)
    params = pltpu.CompilerParams(vmem_limit_bytes=VMEM_LIMIT)
    buffer = jax.ShapeDtypeStruct((local, local, lanes), jnp.bfloat16)

    def field_spec(q):
        return pl.BlockSpec((1, blocks * order, width), lambda g, rank: (0, g, q))

    def factor_spec(size):
        return pl.BlockSpec((size, order, order), lambda g, rank: (g, 0, 0))

    token = jax.ShapeDtypeStruct(TOKEN, jnp.float32)
    token_spec = pl.BlockSpec(TOKEN, lambda g, rank: (0, 0))

    def unread(after):
        return [pl.BlockSpec(memory_space=pl.ANY)] * len(after)

    def left_forward(q, after):
        return pl.pallas_call(
            functools.partial(left_forward_kernel, ranks),
            out_shape=[buffer] * ranks + [token],
            grid_spec=pltpu.PrefetchScalarGridSpec(
                num_scalar_prefetch=1,
                grid=(local // blocks,),
                in_specs=[field_spec(q), field_spec(q), factor_spec(blocks)] + unread(after),
                out_specs=[pl.BlockSpec((blocks, local, lanes), lambda g, rank: (g, 0, 0))] * ranks
                + [token_spec],
            ),
            compiler_params=params,
            cost_estimate=COST,
        )(rank, values, cotangent, left_factor, *after)

    def exchange(sends):
        return [sends[0]] + [
            lax.ppermute(sends[n], "seq", [(r, r ^ moves[n]) for r in range(ranks)])
            for n in range(1, ranks)
        ]

    def right_both(q, arrived, terms, after):
        held = [] if terms is None else [terms]
        moved = pl.BlockSpec((local, rows, lanes), lambda g, rank: (0, g, 0))
        return pl.pallas_call(
            functools.partial(right_kernel, ranks),
            out_shape=[buffer] * ranks
            + [jax.ShapeDtypeStruct((row_count, SHARED * width), jnp.bfloat16), token],
            grid_spec=pltpu.PrefetchScalarGridSpec(
                num_scalar_prefetch=1,
                grid=(local // rows,),
                in_specs=[
                    pl.BlockSpec((rows * order, width), lambda g, rank: (g, q)),
                    factor_spec(rows),
                ]
                + [moved] * ranks
                + unread(held)
                + unread(after),
                out_specs=[moved] * ranks
                + [pl.BlockSpec((rows * order, width), lambda g, rank: (g, q % SHARED)), token_spec],
                scratch_shapes=[
                    pltpu.VMEM((2, order * rows, width), jnp.float32),
                    pltpu.VMEM((2, order * rows, width), jnp.float32),
                ],
            ),
            input_output_aliases={3 + ranks: ranks} if held else {},
            compiler_params=params,
            cost_estimate=COST,
        )(rank, kernel, right_factor, *arrived, *held, *after)

    def left_back(q, arrived, reduced, outputs, after):
        steps = local // blocks
        shard = row_count // groups
        out_shape = [
            jax.ShapeDtypeStruct(values.shape, jnp.bfloat16),
            jax.ShapeDtypeStruct(values.shape, jnp.bfloat16),
            jax.ShapeDtypeStruct((shard, channels), jnp.float32),
            token,
        ]
        earlier = list(outputs) if outputs else []
        terms = len(reduced)
        aliases = {4 + ranks + terms + n: n for n in range(len(earlier))}
        grad_spec = pl.BlockSpec((shard // steps, channels), lambda g, rank: (g, 0))
        return pl.pallas_call(
            functools.partial(left_back_kernel, ranks, terms),
            out_shape=out_shape,
            grid_spec=pltpu.PrefetchScalarGridSpec(
                num_scalar_prefetch=1,
                grid=(steps,),
                in_specs=[
                    field_spec(q),
                    field_spec(q),
                    factor_spec(blocks),
                ]
                + [pl.BlockSpec((blocks, local, lanes), lambda g, rank: (g, 0, 0))] * ranks
                + [pl.BlockSpec((shard // steps, SHARED * width), lambda g, rank: (g, 0))] * terms
                + unread(earlier)
                + unread(after),
                out_specs=[
                    field_spec(q),
                    field_spec(q),
                    grad_spec if terms else pl.BlockSpec(memory_space=pl.ANY),
                    token_spec,
                ],
            ),
            input_output_aliases=aliases,
            compiler_params=params,
            cost_estimate=COST,
        )(rank, values, cotangent, left_factor, *arrived, *reduced, *earlier, *after)

    received, returned = {}, {}
    left_tokens, right_tokens = {}, {}
    reduced, terms, outputs = [], None, None

    for q in range(chunks):
        for n in range(len(left_tokens), min(q + 3, chunks)):
            after = [left_tokens[n - 1]] if n else []
            if n >= 2:
                after += received[n - 2][1:]
            *sends, left_tokens[n] = left_forward(n, after)
            received[n] = exchange(sends)
        after = [right_tokens[q - 1]] if q else []
        if q + 2 in left_tokens:
            after.append(left_tokens[q + 2])
        if q == chunks - 1:
            after += returned[0][1 : 1 + EARLY]
        *sends, terms, right_tokens[q] = right_both(q, received[q], terms, after)
        returned[q] = exchange(sends)
        if (q + 1) % SHARED == 0:
            reduced.append(lax.psum_scatter(terms, "dp", scatter_dimension=0, tiled=True))
            terms = None
    for q in range(chunks):
        last = q == chunks - 1
        outputs = left_back(
            q, returned[q], reduced if last else [], outputs, [right_tokens[chunks - 1]]
        )[:3]
    return tuple(outputs)


def solution(mesh):
    in_specs = (
        P("dp", "seq", None),
        P("dp", "seq", None),
        P("seq", None),
        P("seq", None, None),
        P("seq", None, None),
    )
    out_specs = (P("dp", "seq", None), P("dp", "seq", None), P(("seq", "dp"), None))
    return jax.shard_map(
        functools.partial(per_device, ranks=mesh.shape["seq"], groups=mesh.shape["dp"]),
        mesh=mesh,
        in_specs=in_specs,
        out_specs=out_specs,
        check_vma=False,
    )
```

```python
import functools

import jax
import jax.numpy as jnp
from jax import lax
from jax.experimental import pallas as pl
from jax.experimental.pallas import tpu as pltpu
from jax.sharding import PartitionSpec as P

WIDTH = 128
ROWS = 16
VMEM_LIMIT = 60 * 1024 * 1024
COST = pl.CostEstimate(flops=1024, bytes_accessed=1024, transcendentals=0)
UNROLL = 4
BACK_COST = pl.CostEstimate(flops=40 * 10**9, bytes_accessed=1024, transcendentals=0)
TOKEN = (8, 128)


def moves_of(ranks):
    return [0] + list(range(2, ranks, 2)) + list(range(3, ranks, 2)) + [1]


def left_forward_kernel(ranks, rank_ref, values_ref, cotangent_ref, left_ref, *refs):
    moves = moves_of(ranks)
    *sends, token_ref = refs[-ranks - 1 :]
    token_ref[...] = jnp.zeros_like(token_ref)
    blocks, order, _ = left_ref.shape
    share = order // ranks
    rank = rank_ref[0]
    for i in range(blocks):
        rows = slice(i * order, (i + 1) * order)
        source = values_ref[0, rows, :]
        gated = source.astype(jnp.float32) * cotangent_ref[0, rows, :].astype(jnp.float32)
        both = jnp.concatenate([source, gated.astype(jnp.bfloat16)], axis=1)
        factor = jnp.concatenate(
            [left_ref[i, pl.ds(pl.multiple_of((rank ^ m) * share, share), share), :] for m in moves],
            axis=0,
        )
        first = jnp.dot(factor, both, preferred_element_type=jnp.float32).astype(jnp.bfloat16)
        for m in range(ranks):
            sends[m][i] = first[m * share : (m + 1) * share]


def right_kernel(ranks, rank_ref, kernel_ref, right_ref, *refs):
    arrived = refs[:ranks]
    *sends, term_ref, token_ref, gathered, scattered = refs[-ranks - 4 :]
    token_ref[...] = jnp.zeros_like(token_ref)
    share, rows, lanes = arrived[0].shape
    order = right_ref.shape[1]
    width = lanes // 2
    rank = rank_ref[0]
    halves = [slice(0, width), slice(width, lanes)]

    moves = moves_of(ranks)

    def span(n):
        m = moves[n]
        return pl.ds(pl.multiple_of((rank ^ m) * (share * rows), share * rows), share * rows)

    for m in range(ranks):
        for half in range(2):
            block = arrived[m][:, :, halves[half]].astype(jnp.float32)
            gathered[half, span(m), :] = block.reshape(share * rows, width)

    def step(k, carry):
        both = jnp.concatenate(
            [gathered[half, pl.ds(k, order, stride=rows), :] for half in range(2)], axis=1
        ).astype(jnp.bfloat16)
        factor = right_ref[k]
        result = jnp.dot(factor, both, preferred_element_type=jnp.float32)
        spectrum = result[:, :width].astype(jnp.bfloat16).astype(jnp.float32)
        spectrum_grad = result[:, width:]
        here = pl.ds(pl.multiple_of(k * order, order), order)
        kernel_wide = kernel_ref[here, :].astype(jnp.float32)
        term_ref[here, :] = (spectrum_grad * spectrum).astype(jnp.bfloat16)
        domain = jnp.concatenate(
            [
                (kernel_wide * spectrum).astype(jnp.bfloat16),
                (kernel_wide * spectrum_grad).astype(jnp.bfloat16),
            ],
            axis=1,
        )
        back = lax.dot_general(
            factor, domain, (((0,), (0,)), ((), ())), preferred_element_type=jnp.float32
        )
        for half in range(2):
            scattered[half, pl.ds(k, order, stride=rows), :] = back[:, halves[half]]
        return carry

    def several(g, carry):
        for n in range(UNROLL):
            step(g * UNROLL + n, carry)
        return carry

    lax.fori_loop(0, rows // UNROLL, several, 0)

    for m in range(ranks):
        for half in range(2):
            block = scattered[half, span(m), :].astype(jnp.bfloat16)
            sends[m][:, :, halves[half]] = block.reshape(share, rows, width)


def gate_kernel(*refs):
    pass


def left_back_kernel(ranks, terms, rank_ref, values_ref, cotangent_ref, left_ref, *refs):
    moves = moves_of(ranks)
    arrived, reduced = refs[:ranks], refs[ranks : ranks + terms]
    mixed_ref, values_grad_ref, kernel_grad_ref, token_ref = refs[-4:]
    token_ref[...] = jnp.zeros_like(token_ref)
    blocks, order, _ = left_ref.shape
    share = order // ranks
    width = values_ref.shape[2]
    rank = rank_ref[0]
    for i in range(blocks):
        rows = slice(i * order, (i + 1) * order)
        factor = jnp.concatenate(
            [left_ref[i, pl.ds(pl.multiple_of((rank ^ m) * share, share), share), :] for m in moves],
            axis=0,
        )
        back = jnp.concatenate([arrived[m][i] for m in range(ranks)], axis=0)
        result = lax.dot_general(
            factor, back, (((0,), (0,)), ((), ())), preferred_element_type=jnp.float32
        )
        convolved, carried = result[:, :width], result[:, width:]
        source = values_ref[0, rows, :].astype(jnp.float32)
        upstream = cotangent_ref[0, rows, :].astype(jnp.float32)
        mixed_ref[0, rows, :] = (source * convolved).astype(jnp.bfloat16)
        values_grad_ref[0, rows, :] = (upstream * convolved + carried).astype(jnp.bfloat16)
    for n in range(terms):
        lanes = reduced[n].shape[1]
        kernel_grad_ref[:, n * lanes : (n + 1) * lanes] = reduced[n][...].astype(jnp.float32)


def per_device(values, cotangent, kernel, left_factor, right_factor, ranks, groups):
    sequences, row_count, channels = values.shape
    local, order, _ = left_factor.shape
    width = WIDTH
    lanes = 2 * width
    blocks = min(4, local)
    rows = min(ROWS, local)
    chunks = channels // width
    moves = moves_of(ranks)
    rank = lax.axis_index("seq").astype(jnp.int32).reshape(1)
    params = pltpu.CompilerParams(vmem_limit_bytes=VMEM_LIMIT)
    buffer = jax.ShapeDtypeStruct((local, local, lanes), jnp.bfloat16)

    def field_spec(q):
        return pl.BlockSpec((1, blocks * order, width), lambda g, rank: (0, g, q))

    def factor_spec(size):
        return pl.BlockSpec((size, order, order), lambda g, rank: (g, 0, 0))

    token = jax.ShapeDtypeStruct(TOKEN, jnp.float32)
    token_spec = pl.BlockSpec(TOKEN, lambda g, rank: (0, 0))

    def unread(after):
        return [pl.BlockSpec(memory_space=pl.ANY)] * len(after)

    def left_forward(q, after):
        return pl.pallas_call(
            functools.partial(left_forward_kernel, ranks),
            out_shape=[buffer] * ranks + [token],
            grid_spec=pltpu.PrefetchScalarGridSpec(
                num_scalar_prefetch=1,
                grid=(local // blocks,),
                in_specs=[field_spec(q), field_spec(q), factor_spec(blocks)] + unread(after),
                out_specs=[pl.BlockSpec((blocks, local, lanes), lambda g, rank: (g, 0, 0))] * ranks
                + [token_spec],
            ),
            compiler_params=params,
            cost_estimate=COST,
        )(rank, values, cotangent, left_factor, *after)

    def exchange(sends):
        return [sends[0]] + [
            lax.ppermute(sends[n], "seq", [(r, r ^ moves[n]) for r in range(ranks)])
            for n in range(1, ranks)
        ]

    def right_both(q, arrived, terms, after):
        held = [] if terms is None else [terms]
        moved = pl.BlockSpec((local, rows, lanes), lambda g, rank: (0, g, 0))
        return pl.pallas_call(
            functools.partial(right_kernel, ranks),
            out_shape=[buffer] * ranks
            + [jax.ShapeDtypeStruct((row_count, channels), jnp.bfloat16), token],
            grid_spec=pltpu.PrefetchScalarGridSpec(
                num_scalar_prefetch=1,
                grid=(local // rows,),
                in_specs=[
                    pl.BlockSpec((rows * order, width), lambda g, rank: (g, q)),
                    factor_spec(rows),
                ]
                + [moved] * ranks
                + unread(held)
                + unread(after),
                out_specs=[moved] * ranks
                + [pl.BlockSpec((rows * order, width), lambda g, rank: (g, q)), token_spec],
                scratch_shapes=[
                    pltpu.VMEM((2, order * rows, width), jnp.float32),
                    pltpu.VMEM((2, order * rows, width), jnp.float32),
                ],
            ),
            input_output_aliases={3 + ranks: ranks} if held else {},
            compiler_params=params,
            cost_estimate=COST,
        )(rank, kernel, right_factor, *arrived, *held, *after)

    def gate(sends, after):
        moving = sends[1:]
        return [sends[0]] + list(
            pl.pallas_call(
                gate_kernel,
                out_shape=[buffer] * len(moving),
                in_specs=unread(moving) + unread(after),
                out_specs=unread(moving),
                input_output_aliases={n: n for n in range(len(moving))},
                compiler_params=params,
                cost_estimate=COST,
            )(*moving, *after)
        )

    def left_back(q, arrived, reduced, outputs, after):
        steps = local // blocks
        shard = row_count // groups
        out_shape = [
            jax.ShapeDtypeStruct(values.shape, jnp.bfloat16),
            jax.ShapeDtypeStruct(values.shape, jnp.bfloat16),
            jax.ShapeDtypeStruct((shard, channels), jnp.float32),
            token,
        ]
        earlier = list(outputs) if outputs else []
        terms = len(reduced)
        aliases = {4 + ranks + terms + n: n for n in range(len(earlier))}
        grad_spec = pl.BlockSpec((shard // steps, channels), lambda g, rank: (g, 0))
        return pl.pallas_call(
            functools.partial(left_back_kernel, ranks, terms),
            out_shape=out_shape,
            grid_spec=pltpu.PrefetchScalarGridSpec(
                num_scalar_prefetch=1,
                grid=(steps,),
                in_specs=[
                    field_spec(q),
                    field_spec(q),
                    factor_spec(blocks),
                ]
                + [pl.BlockSpec((blocks, local, lanes), lambda g, rank: (g, 0, 0))] * ranks
                + [pl.BlockSpec((shard // steps, channels), lambda g, rank: (g, 0))] * terms
                + unread(earlier)
                + unread(after),
                out_specs=[
                    field_spec(q),
                    field_spec(q),
                    grad_spec if terms else pl.BlockSpec(memory_space=pl.ANY),
                    token_spec,
                ],
            ),
            input_output_aliases=aliases,
            compiler_params=params,
            cost_estimate=BACK_COST,
        )(rank, values, cotangent, left_factor, *arrived, *reduced, *earlier, *after)

    received, sent, returned = {}, {}, {}
    left_tokens, right_tokens, back_tokens = {}, {}, {}
    terms, outputs = None, []

    def do_left(q):
        after = [left_tokens[q - 1]] if q else []
        if q >= 2:
            after.append(right_tokens[q - 2])
        *sends, left_tokens[q] = left_forward(q, after)
        received[q] = exchange(sends)

    for q in range(min(2, chunks)):
        do_left(q)
    for q in range(chunks):
        after = [right_tokens[q - 1]] if q else []
        *sent[q], terms, right_tokens[q] = right_both(q, received[q], terms, after)
        if q + 2 < chunks:
            do_left(q + 2)
    reduced = lax.psum_scatter(terms, "dp", scatter_dimension=0, tiled=True)

    def back_step(q):
        last = [reduced] if q == chunks - 1 else []
        *outputs[:], back_tokens[q] = left_back(q, returned[q], last, outputs, [right_tokens[chunks - 1]])

    for q in range(chunks):
        after = []
        if 1 <= q < chunks - 1:
            after.append(right_tokens[chunks - 1])
        if q >= 2:
            after.append(back_tokens[q - 2])
        returned[q] = exchange(gate(sent[q], after) if after else sent[q])
        if q >= 1:
            back_step(q - 1)
    back_step(chunks - 1)
    return tuple(outputs)


def solution(mesh):
    in_specs = (
        P("dp", "seq", None),
        P("dp", "seq", None),
        P("seq", None),
        P("seq", None, None),
        P("seq", None, None),
    )
    out_specs = (P("dp", "seq", None), P("dp", "seq", None), P(("seq", "dp"), None))
    return jax.shard_map(
        functools.partial(per_device, ranks=mesh.shape["seq"], groups=mesh.shape["dp"]),
        mesh=mesh,
        in_specs=in_specs,
        out_specs=out_specs,
        check_vma=False,
    )
```

```python
import functools

import jax
import jax.numpy as jnp
from jax import lax
from jax.experimental import pallas as pl
from jax.experimental.pallas import tpu as pltpu
from jax.sharding import PartitionSpec as P

WIDTH = 128
ROWS = 16
VMEM_LIMIT = 60 * 1024 * 1024
COST = pl.CostEstimate(flops=1024, bytes_accessed=1024, transcendentals=0)
EARLY = 3
UNROLL = 4
TOKEN = (8, 128)


def moves_of(ranks):
    return [0] + list(range(2, ranks, 2)) + list(range(3, ranks, 2)) + [1]


def left_forward_kernel(ranks, rank_ref, values_ref, cotangent_ref, left_ref, *refs):
    moves = moves_of(ranks)
    *sends, token_ref = refs[-ranks - 1 :]
    token_ref[...] = jnp.zeros_like(token_ref)
    blocks, order, _ = left_ref.shape
    share = order // ranks
    rank = rank_ref[0]
    for i in range(blocks):
        rows = slice(i * order, (i + 1) * order)
        source = values_ref[0, rows, :]
        gated = source.astype(jnp.float32) * cotangent_ref[0, rows, :].astype(jnp.float32)
        both = jnp.concatenate([source, gated.astype(jnp.bfloat16)], axis=1)
        factor = jnp.concatenate(
            [left_ref[i, pl.ds(pl.multiple_of((rank ^ m) * share, share), share), :] for m in moves],
            axis=0,
        )
        first = jnp.dot(factor, both, preferred_element_type=jnp.float32).astype(jnp.bfloat16)
        for m in range(ranks):
            sends[m][i] = first[m * share : (m + 1) * share]


def right_kernel(ranks, rank_ref, kernel_ref, right_ref, *refs):
    arrived = refs[:ranks]
    *sends, term_ref, token_ref, gathered, scattered = refs[-ranks - 4 :]
    token_ref[...] = jnp.zeros_like(token_ref)
    share, rows, lanes = arrived[0].shape
    order = right_ref.shape[1]
    width = lanes // 2
    rank = rank_ref[0]
    halves = [slice(0, width), slice(width, lanes)]

    moves = moves_of(ranks)

    def span(n):
        m = moves[n]
        return pl.ds(pl.multiple_of((rank ^ m) * (share * rows), share * rows), share * rows)

    for m in range(ranks):
        for half in range(2):
            block = arrived[m][:, :, halves[half]].astype(jnp.float32)
            gathered[half, span(m), :] = block.reshape(share * rows, width)

    def step(k, carry):
        both = jnp.concatenate(
            [gathered[half, pl.ds(k, order, stride=rows), :] for half in range(2)], axis=1
        ).astype(jnp.bfloat16)
        factor = right_ref[k]
        result = jnp.dot(factor, both, preferred_element_type=jnp.float32)
        spectrum = result[:, :width].astype(jnp.bfloat16).astype(jnp.float32)
        spectrum_grad = result[:, width:]
        here = pl.ds(pl.multiple_of(k * order, order), order)
        kernel_wide = kernel_ref[here, :].astype(jnp.float32)
        term_ref[here, :] = (spectrum_grad * spectrum).astype(jnp.bfloat16)
        domain = jnp.concatenate(
            [
                (kernel_wide * spectrum).astype(jnp.bfloat16),
                (kernel_wide * spectrum_grad).astype(jnp.bfloat16),
            ],
            axis=1,
        )
        back = lax.dot_general(
            factor, domain, (((0,), (0,)), ((), ())), preferred_element_type=jnp.float32
        )
        for half in range(2):
            scattered[half, pl.ds(k, order, stride=rows), :] = back[:, halves[half]]
        return carry

    def several(g, carry):
        for n in range(UNROLL):
            step(g * UNROLL + n, carry)
        return carry

    lax.fori_loop(0, rows // UNROLL, several, 0)

    for m in range(ranks):
        for half in range(2):
            block = scattered[half, span(m), :].astype(jnp.bfloat16)
            sends[m][:, :, halves[half]] = block.reshape(share, rows, width)


def gate_kernel(*refs):
    pass


def left_back_kernel(ranks, terms, rank_ref, values_ref, cotangent_ref, left_ref, *refs):
    moves = moves_of(ranks)
    arrived, reduced = refs[:ranks], refs[ranks : ranks + terms]
    mixed_ref, values_grad_ref, kernel_grad_ref, token_ref = refs[-4:]
    token_ref[...] = jnp.zeros_like(token_ref)
    blocks, order, _ = left_ref.shape
    share = order // ranks
    width = values_ref.shape[2]
    rank = rank_ref[0]
    for i in range(blocks):
        rows = slice(i * order, (i + 1) * order)
        factor = jnp.concatenate(
            [left_ref[i, pl.ds(pl.multiple_of((rank ^ m) * share, share), share), :] for m in moves],
            axis=0,
        )
        back = jnp.concatenate([arrived[m][i] for m in range(ranks)], axis=0)
        result = lax.dot_general(
            factor, back, (((0,), (0,)), ((), ())), preferred_element_type=jnp.float32
        )
        convolved, carried = result[:, :width], result[:, width:]
        source = values_ref[0, rows, :].astype(jnp.float32)
        upstream = cotangent_ref[0, rows, :].astype(jnp.float32)
        mixed_ref[0, rows, :] = (source * convolved).astype(jnp.bfloat16)
        values_grad_ref[0, rows, :] = (upstream * convolved + carried).astype(jnp.bfloat16)
    for n in range(terms):
        lanes = reduced[n].shape[1]
        kernel_grad_ref[:, n * lanes : (n + 1) * lanes] = reduced[n][...].astype(jnp.float32)


def per_device(values, cotangent, kernel, left_factor, right_factor, ranks, groups):
    sequences, row_count, channels = values.shape
    local, order, _ = left_factor.shape
    width = WIDTH
    lanes = 2 * width
    blocks = min(4, local)
    rows = min(ROWS, local)
    chunks = channels // width
    moves = moves_of(ranks)
    rank = lax.axis_index("seq").astype(jnp.int32).reshape(1)
    params = pltpu.CompilerParams(vmem_limit_bytes=VMEM_LIMIT)
    buffer = jax.ShapeDtypeStruct((local, local, lanes), jnp.bfloat16)

    def field_spec(q):
        return pl.BlockSpec((1, blocks * order, width), lambda g, rank: (0, g, q))

    def factor_spec(size):
        return pl.BlockSpec((size, order, order), lambda g, rank: (g, 0, 0))

    token = jax.ShapeDtypeStruct(TOKEN, jnp.float32)
    token_spec = pl.BlockSpec(TOKEN, lambda g, rank: (0, 0))

    def unread(after):
        return [pl.BlockSpec(memory_space=pl.ANY)] * len(after)

    def left_forward(q, after):
        return pl.pallas_call(
            functools.partial(left_forward_kernel, ranks),
            out_shape=[buffer] * ranks + [token],
            grid_spec=pltpu.PrefetchScalarGridSpec(
                num_scalar_prefetch=1,
                grid=(local // blocks,),
                in_specs=[field_spec(q), field_spec(q), factor_spec(blocks)] + unread(after),
                out_specs=[pl.BlockSpec((blocks, local, lanes), lambda g, rank: (g, 0, 0))] * ranks
                + [token_spec],
            ),
            compiler_params=params,
            cost_estimate=COST,
        )(rank, values, cotangent, left_factor, *after)

    def exchange(sends):
        return [sends[0]] + [
            lax.ppermute(sends[n], "seq", [(r, r ^ moves[n]) for r in range(ranks)])
            for n in range(1, ranks)
        ]

    def right_both(q, arrived, terms, after):
        held = [] if terms is None else [terms]
        moved = pl.BlockSpec((local, rows, lanes), lambda g, rank: (0, g, 0))
        return pl.pallas_call(
            functools.partial(right_kernel, ranks),
            out_shape=[buffer] * ranks
            + [jax.ShapeDtypeStruct((row_count, channels), jnp.bfloat16), token],
            grid_spec=pltpu.PrefetchScalarGridSpec(
                num_scalar_prefetch=1,
                grid=(local // rows,),
                in_specs=[
                    pl.BlockSpec((rows * order, width), lambda g, rank: (g, q)),
                    factor_spec(rows),
                ]
                + [moved] * ranks
                + unread(held)
                + unread(after),
                out_specs=[moved] * ranks
                + [pl.BlockSpec((rows * order, width), lambda g, rank: (g, q)), token_spec],
                scratch_shapes=[
                    pltpu.VMEM((2, order * rows, width), jnp.float32),
                    pltpu.VMEM((2, order * rows, width), jnp.float32),
                ],
            ),
            input_output_aliases={3 + ranks: ranks} if held else {},
            compiler_params=params,
            cost_estimate=COST,
        )(rank, kernel, right_factor, *arrived, *held, *after)

    def gate(held, after):
        return list(
            pl.pallas_call(
                gate_kernel,
                out_shape=[jax.ShapeDtypeStruct(x.shape, x.dtype) for x in held],
                in_specs=unread(held) + unread(after),
                out_specs=unread(held),
                input_output_aliases={n: n for n in range(len(held))},
                compiler_params=params,
                cost_estimate=COST,
            )(*held, *after)
        )

    def left_back(q, arrived, reduced, outputs, after):
        steps = local // blocks
        shard = row_count // groups
        out_shape = [
            jax.ShapeDtypeStruct(values.shape, jnp.bfloat16),
            jax.ShapeDtypeStruct(values.shape, jnp.bfloat16),
            jax.ShapeDtypeStruct((shard, channels), jnp.float32),
            token,
        ]
        earlier = list(outputs) if outputs else []
        terms = len(reduced)
        aliases = {4 + ranks + terms + n: n for n in range(len(earlier))}
        grad_spec = pl.BlockSpec((shard // steps, channels), lambda g, rank: (g, 0))
        return pl.pallas_call(
            functools.partial(left_back_kernel, ranks, terms),
            out_shape=out_shape,
            grid_spec=pltpu.PrefetchScalarGridSpec(
                num_scalar_prefetch=1,
                grid=(steps,),
                in_specs=[
                    field_spec(q),
                    field_spec(q),
                    factor_spec(blocks),
                ]
                + [pl.BlockSpec((blocks, local, lanes), lambda g, rank: (g, 0, 0))] * ranks
                + [pl.BlockSpec((shard // steps, channels), lambda g, rank: (g, 0))] * terms
                + unread(earlier)
                + unread(after),
                out_specs=[
                    field_spec(q),
                    field_spec(q),
                    grad_spec if terms else pl.BlockSpec(memory_space=pl.ANY),
                    token_spec,
                ],
            ),
            input_output_aliases=aliases,
            compiler_params=params,
            cost_estimate=COST,
        )(rank, values, cotangent, left_factor, *arrived, *reduced, *earlier, *after)

    received, sent, returned = {}, {}, {}
    left_tokens, right_tokens, back_tokens = {}, {}, {}
    terms, outputs = None, []

    def do_left(q):
        after = [left_tokens[q - 1]] if q else []
        if q >= 2:
            after.append(right_tokens[q - 2])
        *sends, left_tokens[q] = left_forward(q, after)
        received[q] = exchange(sends)

    for q in range(min(2, chunks)):
        do_left(q)
    for q in range(chunks):
        after = [right_tokens[q - 1]] if q else []
        *sent[q], terms, right_tokens[q] = right_both(q, received[q], terms, after)
        if q + 2 < chunks:
            do_left(q + 2)

    def back_step(q):
        last = [reduced] if q == chunks - 1 else []
        *outputs[:], back_tokens[q] = left_back(q, returned[q], last, outputs, [right_tokens[chunks - 1]])

    for q in range(chunks):
        after = []
        if 1 <= q < chunks - 1:
            after.append(right_tokens[chunks - 1])
        if q >= 2:
            after.append(back_tokens[q - 2])
        returned[q] = exchange(sent[q][:1] + gate(sent[q][1:], after) if after else sent[q])
        if q == 0:
            (terms,) = gate([terms], returned[0][1 : 1 + EARLY])
            reduced = lax.psum_scatter(terms, "dp", scatter_dimension=0, tiled=True)
        if q >= 1:
            back_step(q - 1)
    back_step(chunks - 1)
    return tuple(outputs)


def solution(mesh):
    in_specs = (
        P("dp", "seq", None),
        P("dp", "seq", None),
        P("seq", None),
        P("seq", None, None),
        P("seq", None, None),
    )
    out_specs = (P("dp", "seq", None), P("dp", "seq", None), P(("seq", "dp"), None))
    return jax.shard_map(
        functools.partial(per_device, ranks=mesh.shape["seq"], groups=mesh.shape["dp"]),
        mesh=mesh,
        in_specs=in_specs,
        out_specs=out_specs,
        check_vma=False,
    )
```

```python
import functools

import jax
import jax.numpy as jnp
from jax import lax
from jax.experimental import pallas as pl
from jax.experimental.pallas import tpu as pltpu
from jax.sharding import PartitionSpec as P

WIDTH = 128
ROWS = 16
VMEM_LIMIT = 60 * 1024 * 1024
COST = pl.CostEstimate(flops=1024, bytes_accessed=1024, transcendentals=0)
EARLY = 3
UNROLL = 4
TOKEN = (8, 128)


def moves_of(ranks):
    return [0] + list(range(2, ranks, 2)) + list(range(3, ranks, 2)) + [1]


def left_forward_kernel(ranks, rank_ref, values_ref, cotangent_ref, left_ref, *refs):
    moves = moves_of(ranks)
    *sends, token_ref = refs[-ranks - 1 :]
    token_ref[...] = jnp.zeros_like(token_ref)
    blocks, order, _ = left_ref.shape
    share = order // ranks
    rank = rank_ref[0]
    for i in range(blocks):
        rows = slice(i * order, (i + 1) * order)
        source = values_ref[0, rows, :]
        gated = source.astype(jnp.float32) * cotangent_ref[0, rows, :].astype(jnp.float32)
        both = jnp.concatenate([source, gated.astype(jnp.bfloat16)], axis=1)
        factor = jnp.concatenate(
            [left_ref[i, pl.ds(pl.multiple_of((rank ^ m) * share, share), share), :] for m in moves],
            axis=0,
        )
        first = jnp.dot(factor, both, preferred_element_type=jnp.float32).astype(jnp.bfloat16)
        for m in range(ranks):
            sends[m][i] = first[m * share : (m + 1) * share]


def right_kernel(ranks, rank_ref, kernel_ref, right_ref, *refs):
    arrived = refs[:ranks]
    *sends, term_ref, token_ref, gathered, scattered = refs[-ranks - 4 :]
    token_ref[...] = jnp.zeros_like(token_ref)
    share, rows, lanes = arrived[0].shape
    order = right_ref.shape[1]
    width = lanes // 2
    rank = rank_ref[0]
    halves = [slice(0, width), slice(width, lanes)]

    moves = moves_of(ranks)

    def span(n):
        m = moves[n]
        return pl.ds(pl.multiple_of((rank ^ m) * (share * rows), share * rows), share * rows)

    for m in range(ranks):
        for half in range(2):
            block = arrived[m][:, :, halves[half]].astype(jnp.float32)
            gathered[half, span(m), :] = block.reshape(share * rows, width)

    def step(k, carry):
        both = jnp.concatenate(
            [gathered[half, pl.ds(k, order, stride=rows), :] for half in range(2)], axis=1
        ).astype(jnp.bfloat16)
        factor = right_ref[k]
        result = jnp.dot(factor, both, preferred_element_type=jnp.float32)
        spectrum = result[:, :width].astype(jnp.bfloat16).astype(jnp.float32)
        spectrum_grad = result[:, width:]
        here = pl.ds(pl.multiple_of(k * order, order), order)
        kernel_wide = kernel_ref[here, :].astype(jnp.float32)
        term_ref[here, :] = (spectrum_grad * spectrum).astype(jnp.bfloat16)
        domain = jnp.concatenate(
            [
                (kernel_wide * spectrum).astype(jnp.bfloat16),
                (kernel_wide * spectrum_grad).astype(jnp.bfloat16),
            ],
            axis=1,
        )
        back = lax.dot_general(
            factor, domain, (((0,), (0,)), ((), ())), preferred_element_type=jnp.float32
        )
        for half in range(2):
            scattered[half, pl.ds(k, order, stride=rows), :] = back[:, halves[half]]
        return carry

    def several(g, carry):
        for n in range(UNROLL):
            step(g * UNROLL + n, carry)
        return carry

    lax.fori_loop(0, rows // UNROLL, several, 0)

    for m in range(ranks):
        for half in range(2):
            block = scattered[half, span(m), :].astype(jnp.bfloat16)
            sends[m][:, :, halves[half]] = block.reshape(share, rows, width)


def gate_kernel(*refs):
    pass


def left_back_kernel(ranks, terms, rank_ref, values_ref, cotangent_ref, left_ref, *refs):
    moves = moves_of(ranks)
    arrived, reduced = refs[:ranks], refs[ranks : ranks + terms]
    mixed_ref, values_grad_ref, kernel_grad_ref, token_ref = refs[-4:]
    token_ref[...] = jnp.zeros_like(token_ref)
    blocks, order, _ = left_ref.shape
    share = order // ranks
    width = values_ref.shape[2]
    rank = rank_ref[0]
    for i in range(blocks):
        rows = slice(i * order, (i + 1) * order)
        factor = jnp.concatenate(
            [left_ref[i, pl.ds(pl.multiple_of((rank ^ m) * share, share), share), :] for m in moves],
            axis=0,
        )
        back = jnp.concatenate([arrived[m][i] for m in range(ranks)], axis=0)
        result = lax.dot_general(
            factor, back, (((0,), (0,)), ((), ())), preferred_element_type=jnp.float32
        )
        convolved, carried = result[:, :width], result[:, width:]
        source = values_ref[0, rows, :].astype(jnp.float32)
        upstream = cotangent_ref[0, rows, :].astype(jnp.float32)
        mixed_ref[0, rows, :] = (source * convolved).astype(jnp.bfloat16)
        values_grad_ref[0, rows, :] = (upstream * convolved + carried).astype(jnp.bfloat16)
    for n in range(terms):
        lanes = reduced[n].shape[1]
        kernel_grad_ref[:, n * lanes : (n + 1) * lanes] = reduced[n][...].astype(jnp.float32)


def per_device(values, cotangent, kernel, left_factor, right_factor, ranks, groups):
    sequences, row_count, channels = values.shape
    local, order, _ = left_factor.shape
    width = WIDTH
    lanes = 2 * width
    blocks = min(4, local)
    rows = min(ROWS, local)
    chunks = channels // width
    moves = moves_of(ranks)
    rank = lax.axis_index("seq").astype(jnp.int32).reshape(1)
    params = pltpu.CompilerParams(vmem_limit_bytes=VMEM_LIMIT)
    buffer = jax.ShapeDtypeStruct((local, local, lanes), jnp.bfloat16)

    def field_spec(q):
        return pl.BlockSpec((1, blocks * order, width), lambda g, rank: (0, g, q))

    def factor_spec(size):
        return pl.BlockSpec((size, order, order), lambda g, rank: (g, 0, 0))

    token = jax.ShapeDtypeStruct(TOKEN, jnp.float32)
    token_spec = pl.BlockSpec(TOKEN, lambda g, rank: (0, 0))

    def unread(after):
        return [pl.BlockSpec(memory_space=pl.ANY)] * len(after)

    def left_forward(q, after):
        return pl.pallas_call(
            functools.partial(left_forward_kernel, ranks),
            out_shape=[buffer] * ranks + [token],
            grid_spec=pltpu.PrefetchScalarGridSpec(
                num_scalar_prefetch=1,
                grid=(local // blocks,),
                in_specs=[field_spec(q), field_spec(q), factor_spec(blocks)] + unread(after),
                out_specs=[pl.BlockSpec((blocks, local, lanes), lambda g, rank: (g, 0, 0))] * ranks
                + [token_spec],
            ),
            compiler_params=params,
            cost_estimate=COST,
        )(rank, values, cotangent, left_factor, *after)

    def exchange(sends):
        return [sends[0]] + [
            lax.ppermute(sends[n], "seq", [(r, r ^ moves[n]) for r in range(ranks)])
            for n in range(1, ranks)
        ]

    def right_both(q, arrived, terms, after):
        held = [] if terms is None else [terms]
        moved = pl.BlockSpec((local, rows, lanes), lambda g, rank: (0, g, 0))
        return pl.pallas_call(
            functools.partial(right_kernel, ranks),
            out_shape=[buffer] * ranks
            + [jax.ShapeDtypeStruct((row_count, channels), jnp.bfloat16), token],
            grid_spec=pltpu.PrefetchScalarGridSpec(
                num_scalar_prefetch=1,
                grid=(local // rows,),
                in_specs=[
                    pl.BlockSpec((rows * order, width), lambda g, rank: (g, q)),
                    factor_spec(rows),
                ]
                + [moved] * ranks
                + unread(held)
                + unread(after),
                out_specs=[moved] * ranks
                + [pl.BlockSpec((rows * order, width), lambda g, rank: (g, q)), token_spec],
                scratch_shapes=[
                    pltpu.VMEM((2, order * rows, width), jnp.float32),
                    pltpu.VMEM((2, order * rows, width), jnp.float32),
                ],
            ),
            input_output_aliases={3 + ranks: ranks} if held else {},
            compiler_params=params,
            cost_estimate=COST,
        )(rank, kernel, right_factor, *arrived, *held, *after)

    def gate(held, after):
        return list(
            pl.pallas_call(
                gate_kernel,
                out_shape=[jax.ShapeDtypeStruct(x.shape, x.dtype) for x in held],
                in_specs=unread(held) + unread(after),
                out_specs=unread(held),
                input_output_aliases={n: n for n in range(len(held))},
                compiler_params=params,
                cost_estimate=COST,
            )(*held, *after)
        )

    def left_back(q, arrived, reduced, outputs, after):
        steps = local // blocks
        shard = row_count // groups
        out_shape = [
            jax.ShapeDtypeStruct(values.shape, jnp.bfloat16),
            jax.ShapeDtypeStruct(values.shape, jnp.bfloat16),
            jax.ShapeDtypeStruct((shard, channels), jnp.float32),
            token,
        ]
        earlier = list(outputs) if outputs else []
        terms = len(reduced)
        aliases = {4 + ranks + terms + n: n for n in range(len(earlier))}
        grad_spec = pl.BlockSpec((shard // steps, channels), lambda g, rank: (g, 0))
        return pl.pallas_call(
            functools.partial(left_back_kernel, ranks, terms),
            out_shape=out_shape,
            grid_spec=pltpu.PrefetchScalarGridSpec(
                num_scalar_prefetch=1,
                grid=(steps,),
                in_specs=[
                    field_spec(q),
                    field_spec(q),
                    factor_spec(blocks),
                ]
                + [pl.BlockSpec((blocks, local, lanes), lambda g, rank: (g, 0, 0))] * ranks
                + [pl.BlockSpec((shard // steps, channels), lambda g, rank: (g, 0))] * terms
                + unread(earlier)
                + unread(after),
                out_specs=[
                    field_spec(q),
                    field_spec(q),
                    grad_spec if terms else pl.BlockSpec(memory_space=pl.ANY),
                    token_spec,
                ],
            ),
            input_output_aliases=aliases,
            compiler_params=params,
            cost_estimate=COST,
        )(rank, values, cotangent, left_factor, *arrived, *reduced, *earlier, *after)

    received, sent, returned = {}, {}, {}
    left_tokens, right_tokens, back_tokens = {}, {}, {}
    terms, outputs = None, []

    parts = {}
    for q in range(chunks):
        *parts[q], left_tokens[q] = left_forward(q, [left_tokens[q - 1]] if q else [])

    def send_left(q):
        sends = parts[q]
        after = []
        if q == 1:
            after.append(left_tokens[chunks - 1])
        if q >= 2:
            after.append(right_tokens[q - 2])
        if after:
            sends[1 + EARLY :] = gate(sends[1 + EARLY :], after)
        received[q] = exchange(sends)

    for q in range(min(2, chunks)):
        send_left(q)
    for q in range(chunks):
        after = [right_tokens[q - 1]] if q else []
        *sent[q], terms, right_tokens[q] = right_both(q, received[q], terms, after)
        if q + 2 < chunks:
            send_left(q + 2)

    def back_step(q):
        last = [reduced] if q == chunks - 1 else []
        *outputs[:], back_tokens[q] = left_back(q, returned[q], last, outputs, [right_tokens[chunks - 1]])

    for q in range(chunks):
        after = []
        if 1 <= q < chunks - 1:
            after.append(right_tokens[chunks - 1])
        if q >= 2:
            after.append(back_tokens[q - 2])
        sends = list(sent[q])
        if q == 0 and chunks > 2:
            sends[1 : 1 + EARLY] = gate(sends[1 : 1 + EARLY], [right_tokens[chunks - 2]])
        if after:
            sends[1:] = gate(sends[1:], after)
        returned[q] = exchange(sends)
        if q == 0:
            (terms,) = gate([terms], returned[0][1 : 1 + EARLY])
            reduced = lax.psum_scatter(terms, "dp", scatter_dimension=0, tiled=True)
        if q >= 1:
            back_step(q - 1)
    back_step(chunks - 1)
    return tuple(outputs)


def solution(mesh):
    in_specs = (
        P("dp", "seq", None),
        P("dp", "seq", None),
        P("seq", None),
        P("seq", None, None),
        P("seq", None, None),
    )
    out_specs = (P("dp", "seq", None), P("dp", "seq", None), P(("seq", "dp"), None))
    return jax.shard_map(
        functools.partial(per_device, ranks=mesh.shape["seq"], groups=mesh.shape["dp"]),
        mesh=mesh,
        in_specs=in_specs,
        out_specs=out_specs,
        check_vma=False,
    )
```

```python
import functools

import jax
import jax.numpy as jnp
from jax import lax
from jax.experimental import pallas as pl
from jax.experimental.pallas import tpu as pltpu
from jax.sharding import PartitionSpec as P

WIDTH = 128
ROWS = 16
VMEM_LIMIT = 60 * 1024 * 1024
COST = pl.CostEstimate(flops=1024, bytes_accessed=1024, transcendentals=0)
EARLY = 3
UNROLL = 4
TOKEN = (8, 128)


def moves_of(ranks):
    return [0] + list(range(2, ranks, 2)) + list(range(3, ranks, 2)) + [1]


def left_forward_kernel(ranks, rank_ref, values_ref, cotangent_ref, left_ref, *refs):
    moves = moves_of(ranks)
    *sends, token_ref = refs[-ranks - 1 :]
    token_ref[...] = jnp.zeros_like(token_ref)
    blocks, order, _ = left_ref.shape
    share = order // ranks
    rank = rank_ref[0]
    for i in range(blocks):
        rows = slice(i * order, (i + 1) * order)
        source = values_ref[0, rows, :]
        gated = source.astype(jnp.float32) * cotangent_ref[0, rows, :].astype(jnp.float32)
        both = jnp.concatenate([source, gated.astype(jnp.bfloat16)], axis=1)
        factor = jnp.concatenate(
            [left_ref[i, pl.ds(pl.multiple_of((rank ^ m) * share, share), share), :] for m in moves],
            axis=0,
        )
        first = jnp.dot(factor, both, preferred_element_type=jnp.float32).astype(jnp.bfloat16)
        for m in range(ranks):
            sends[m][i] = first[m * share : (m + 1) * share]


def right_kernel(ranks, rank_ref, kernel_ref, right_ref, *refs):
    arrived = refs[:ranks]
    *sends, term_ref, token_ref, gathered, scattered = refs[-ranks - 4 :]
    token_ref[...] = jnp.zeros_like(token_ref)
    share, rows, lanes = arrived[0].shape
    order = right_ref.shape[1]
    width = lanes // 2
    rank = rank_ref[0]
    halves = [slice(0, width), slice(width, lanes)]

    moves = moves_of(ranks)

    def span(n):
        m = moves[n]
        return pl.ds(pl.multiple_of((rank ^ m) * (share * rows), share * rows), share * rows)

    for m in range(ranks):
        for half in range(2):
            block = arrived[m][:, :, halves[half]].astype(jnp.float32)
            gathered[half, span(m), :] = block.reshape(share * rows, width)

    def step(k, carry):
        both = jnp.concatenate(
            [gathered[half, pl.ds(k, order, stride=rows), :] for half in range(2)], axis=1
        ).astype(jnp.bfloat16)
        factor = right_ref[k]
        result = jnp.dot(factor, both, preferred_element_type=jnp.float32)
        spectrum = result[:, :width].astype(jnp.bfloat16).astype(jnp.float32)
        spectrum_grad = result[:, width:]
        here = pl.ds(pl.multiple_of(k * order, order), order)
        kernel_wide = kernel_ref[here, :].astype(jnp.float32)
        term_ref[here, :] = (spectrum_grad * spectrum).astype(jnp.bfloat16)
        domain = jnp.concatenate(
            [
                (kernel_wide * spectrum).astype(jnp.bfloat16),
                (kernel_wide * spectrum_grad).astype(jnp.bfloat16),
            ],
            axis=1,
        )
        back = lax.dot_general(
            factor, domain, (((0,), (0,)), ((), ())), preferred_element_type=jnp.float32
        )
        for half in range(2):
            scattered[half, pl.ds(k, order, stride=rows), :] = back[:, halves[half]]
        return carry

    def several(g, carry):
        for n in range(UNROLL):
            step(g * UNROLL + n, carry)
        return carry

    lax.fori_loop(0, rows // UNROLL, several, 0)

    for m in range(ranks):
        for half in range(2):
            block = scattered[half, span(m), :].astype(jnp.bfloat16)
            sends[m][:, :, halves[half]] = block.reshape(share, rows, width)


def gate_kernel(*refs):
    pass


def left_back_kernel(ranks, terms, rank_ref, values_ref, cotangent_ref, left_ref, *refs):
    moves = moves_of(ranks)
    arrived, reduced = refs[:ranks], refs[ranks : ranks + terms]
    mixed_ref, values_grad_ref, kernel_grad_ref, token_ref = refs[-4:]
    token_ref[...] = jnp.zeros_like(token_ref)
    blocks, order, _ = left_ref.shape
    share = order // ranks
    width = values_ref.shape[2]
    rank = rank_ref[0]
    for i in range(blocks):
        rows = slice(i * order, (i + 1) * order)
        factor = jnp.concatenate(
            [left_ref[i, pl.ds(pl.multiple_of((rank ^ m) * share, share), share), :] for m in moves],
            axis=0,
        )
        back = jnp.concatenate([arrived[m][i] for m in range(ranks)], axis=0)
        result = lax.dot_general(
            factor, back, (((0,), (0,)), ((), ())), preferred_element_type=jnp.float32
        )
        convolved, carried = result[:, :width], result[:, width:]
        source = values_ref[0, rows, :].astype(jnp.float32)
        upstream = cotangent_ref[0, rows, :].astype(jnp.float32)
        mixed_ref[0, rows, :] = (source * convolved).astype(jnp.bfloat16)
        values_grad_ref[0, rows, :] = (upstream * convolved + carried).astype(jnp.bfloat16)
    for n in range(terms):
        lanes = reduced[n].shape[1]
        kernel_grad_ref[:, n * lanes : (n + 1) * lanes] = reduced[n][...].astype(jnp.float32)


def per_device(values, cotangent, kernel, left_factor, right_factor, ranks, groups):
    sequences, row_count, channels = values.shape
    local, order, _ = left_factor.shape
    width = WIDTH
    lanes = 2 * width
    blocks = min(4, local)
    rows = min(ROWS, local)
    chunks = channels // width
    moves = moves_of(ranks)
    rank = lax.axis_index("seq").astype(jnp.int32).reshape(1)
    params = pltpu.CompilerParams(vmem_limit_bytes=VMEM_LIMIT)
    together = [[0], list(range(1, chunks - 1)), [chunks - 1]]
    group_of = {q: members for members in together for q in members}

    def buffer(q):
        return jax.ShapeDtypeStruct((local, local, len(group_of[q]) * lanes), jnp.bfloat16)

    def place(q):
        return group_of[q].index(q)

    def field_spec(q):
        return pl.BlockSpec((1, blocks * order, width), lambda g, rank: (0, g, q))

    def factor_spec(size):
        return pl.BlockSpec((size, order, order), lambda g, rank: (g, 0, 0))

    token = jax.ShapeDtypeStruct(TOKEN, jnp.float32)
    token_spec = pl.BlockSpec(TOKEN, lambda g, rank: (0, 0))

    def unread(after):
        return [pl.BlockSpec(memory_space=pl.ANY)] * len(after)

    def left_forward(q, held, after):
        return pl.pallas_call(
            functools.partial(left_forward_kernel, ranks),
            out_shape=[buffer(q)] * ranks + [token],
            grid_spec=pltpu.PrefetchScalarGridSpec(
                num_scalar_prefetch=1,
                grid=(local // blocks,),
                in_specs=[field_spec(q), field_spec(q), factor_spec(blocks)]
                + unread(held)
                + unread(after),
                out_specs=[pl.BlockSpec((blocks, local, lanes), lambda g, rank: (g, 0, place(q)))] * ranks
                + [token_spec],
            ),
            input_output_aliases={4 + n: n for n in range(len(held))},
            compiler_params=params,
            cost_estimate=COST,
        )(rank, values, cotangent, left_factor, *held, *after)

    def exchange(sends):
        return [sends[0]] + [
            lax.ppermute(sends[n], "seq", [(r, r ^ moves[n]) for r in range(ranks)])
            for n in range(1, ranks)
        ]

    def right_both(q, arrived, terms, held, after):
        earlier = [] if terms is None else [terms]
        aliases = {3 + ranks: ranks} if earlier else {}
        aliases.update({3 + ranks + len(earlier) + n: n for n in range(len(held))})
        moved = pl.BlockSpec((local, rows, lanes), lambda g, rank: (0, g, place(q)))
        return pl.pallas_call(
            functools.partial(right_kernel, ranks),
            out_shape=[buffer(q)] * ranks
            + [jax.ShapeDtypeStruct((row_count, channels), jnp.bfloat16), token],
            grid_spec=pltpu.PrefetchScalarGridSpec(
                num_scalar_prefetch=1,
                grid=(local // rows,),
                in_specs=[
                    pl.BlockSpec((rows * order, width), lambda g, rank: (g, q)),
                    factor_spec(rows),
                ]
                + [moved] * ranks
                + unread(earlier)
                + unread(held)
                + unread(after),
                out_specs=[moved] * ranks
                + [pl.BlockSpec((rows * order, width), lambda g, rank: (g, q)), token_spec],
                scratch_shapes=[
                    pltpu.VMEM((2, order * rows, width), jnp.float32),
                    pltpu.VMEM((2, order * rows, width), jnp.float32),
                ],
            ),
            input_output_aliases=aliases,
            compiler_params=params,
            cost_estimate=COST,
        )(rank, kernel, right_factor, *arrived, *earlier, *held, *after)

    def gate(held, after):
        return list(
            pl.pallas_call(
                gate_kernel,
                out_shape=[jax.ShapeDtypeStruct(x.shape, x.dtype) for x in held],
                in_specs=unread(held) + unread(after),
                out_specs=unread(held),
                input_output_aliases={n: n for n in range(len(held))},
                compiler_params=params,
                cost_estimate=COST,
            )(*held, *after)
        )

    def left_back(q, arrived, reduced, outputs, after):
        steps = local // blocks
        shard = row_count // groups
        out_shape = [
            jax.ShapeDtypeStruct(values.shape, jnp.bfloat16),
            jax.ShapeDtypeStruct(values.shape, jnp.bfloat16),
            jax.ShapeDtypeStruct((shard, channels), jnp.float32),
            token,
        ]
        earlier = list(outputs) if outputs else []
        terms = len(reduced)
        aliases = {4 + ranks + terms + n: n for n in range(len(earlier))}
        grad_spec = pl.BlockSpec((shard // steps, channels), lambda g, rank: (g, 0))
        return pl.pallas_call(
            functools.partial(left_back_kernel, ranks, terms),
            out_shape=out_shape,
            grid_spec=pltpu.PrefetchScalarGridSpec(
                num_scalar_prefetch=1,
                grid=(steps,),
                in_specs=[
                    field_spec(q),
                    field_spec(q),
                    factor_spec(blocks),
                ]
                + [pl.BlockSpec((blocks, local, lanes), lambda g, rank: (g, 0, place(q)))] * ranks
                + [pl.BlockSpec((shard // steps, channels), lambda g, rank: (g, 0))] * terms
                + unread(earlier)
                + unread(after),
                out_specs=[
                    field_spec(q),
                    field_spec(q),
                    grad_spec if terms else pl.BlockSpec(memory_space=pl.ANY),
                    token_spec,
                ],
            ),
            input_output_aliases=aliases,
            compiler_params=params,
            cost_estimate=COST,
        )(rank, values, cotangent, left_factor, *arrived, *reduced, *earlier, *after)

    received, returned = [], []
    left_tokens, right_tokens, back_tokens = {}, {}, {}
    terms, outputs = None, []

    parts, sent = [[] for _ in together], [[] for _ in together]
    for n, members in enumerate(together):
        for q in members:
            *parts[n], left_tokens[q] = left_forward(q, parts[n], [left_tokens[q - 1]] if q else [])

    def middle(n, q):
        nonlocal terms
        after = [right_tokens[q - 1]] if q else []
        *sent[n], terms, right_tokens[q] = right_both(q, received[n], terms, sent[n], after)

    def back(n, q):
        last = [reduced] if q == chunks - 1 else []
        *outputs[:], back_tokens[q] = left_back(q, returned[n], last, outputs, [right_tokens[chunks - 1]])

    received.append(exchange(parts[0]))
    middle(0, 0)
    parts[1][1 + EARLY :] = gate(parts[1][1 + EARLY :], [left_tokens[chunks - 1], right_tokens[0]])
    received.append(exchange(parts[1]))
    middle(1, 1)
    parts[2][1 + EARLY :] = gate(parts[2][1 + EARLY :], [right_tokens[1]])
    received.append(exchange(parts[2]))
    for q in together[1][1:]:
        middle(1, q)
    sent[0][1 : 1 + EARLY] = gate(sent[0][1 : 1 + EARLY], [right_tokens[chunks - 2]])
    returned.append(exchange(sent[0]))
    middle(2, chunks - 1)
    (terms,) = gate([terms], returned[0][1 : 1 + EARLY])
    reduced = lax.psum_scatter(terms, "dp", scatter_dimension=0, tiled=True)
    sent[1][1:] = gate(sent[1][1:], [right_tokens[chunks - 1]])
    returned.append(exchange(sent[1]))
    back(0, 0)
    sent[2][1:] = gate(sent[2][1:], [back_tokens[0]])
    returned.append(exchange(sent[2]))
    for q in together[1]:
        back(1, q)
    back(2, chunks - 1)
    return tuple(outputs)


def solution(mesh):
    in_specs = (
        P("dp", "seq", None),
        P("dp", "seq", None),
        P("seq", None),
        P("seq", None, None),
        P("seq", None, None),
    )
    out_specs = (P("dp", "seq", None), P("dp", "seq", None), P(("seq", "dp"), None))
    return jax.shard_map(
        functools.partial(per_device, ranks=mesh.shape["seq"], groups=mesh.shape["dp"]),
        mesh=mesh,
        in_specs=in_specs,
        out_specs=out_specs,
        check_vma=False,
    )
```

```python
import functools

import jax
import jax.numpy as jnp
from jax import lax
from jax.experimental import pallas as pl
from jax.experimental.pallas import tpu as pltpu
from jax.sharding import PartitionSpec as P

WIDTH = 128
ROWS = 16
VMEM_LIMIT = 60 * 1024 * 1024
COST = pl.CostEstimate(flops=1024, bytes_accessed=1024, transcendentals=0)
FIRST = 5
EARLY = 3
UNROLL = 4
TOKEN = (8, 128)


def moves_of(ranks):
    return [0] + list(range(2, ranks, 2)) + list(range(3, ranks, 2)) + [1]


def left_forward_kernel(ranks, rank_ref, values_ref, cotangent_ref, left_ref, *refs):
    moves = moves_of(ranks)
    *sends, token_ref = refs[-ranks - 1 :]
    token_ref[...] = jnp.zeros_like(token_ref)
    blocks, order, _ = left_ref.shape
    share = order // ranks
    rank = rank_ref[0]
    for i in range(blocks):
        rows = slice(i * order, (i + 1) * order)
        source = values_ref[0, rows, :]
        gated = source.astype(jnp.float32) * cotangent_ref[0, rows, :].astype(jnp.float32)
        both = jnp.concatenate([source, gated.astype(jnp.bfloat16)], axis=1)
        factor = jnp.concatenate(
            [left_ref[i, pl.ds(pl.multiple_of((rank ^ m) * share, share), share), :] for m in moves],
            axis=0,
        )
        first = jnp.dot(factor, both, preferred_element_type=jnp.float32).astype(jnp.bfloat16)
        for m in range(ranks):
            sends[m][i] = first[m * share : (m + 1) * share]


def right_kernel(ranks, arrived_parts, sent_parts, rank_ref, kernel_ref, right_ref, *refs):
    arrived = refs[: arrived_parts * ranks]
    *sends, term_ref, token_ref, gathered, scattered = refs[-sent_parts * ranks - 4 :]
    token_ref[...] = jnp.zeros_like(token_ref)
    _, rows, lanes = arrived[0].shape
    order = right_ref.shape[1]
    share = order // ranks
    width = lanes // 2
    rank = rank_ref[0]
    halves = [slice(0, width), slice(width, lanes)]

    moves = moves_of(ranks)

    def span(n, part, parts):
        size = share * rows // parts
        start = (rank ^ moves[n]) * (share * rows) + part * size
        return pl.ds(pl.multiple_of(start, size), size)

    for n, block_ref in enumerate(arrived):
        where = span(n % ranks, n // ranks, arrived_parts)
        for half in range(2):
            block = block_ref[:, :, halves[half]].astype(jnp.float32)
            gathered[half, where, :] = block.reshape(where.size, width)

    def step(k, carry):
        both = jnp.concatenate(
            [gathered[half, pl.ds(k, order, stride=rows), :] for half in range(2)], axis=1
        ).astype(jnp.bfloat16)
        factor = right_ref[k]
        result = jnp.dot(factor, both, preferred_element_type=jnp.float32)
        spectrum = result[:, :width].astype(jnp.bfloat16).astype(jnp.float32)
        spectrum_grad = result[:, width:]
        here = pl.ds(pl.multiple_of(k * order, order), order)
        kernel_wide = kernel_ref[here, :].astype(jnp.float32)
        term_ref[here, :] = (spectrum_grad * spectrum).astype(jnp.bfloat16)
        domain = jnp.concatenate(
            [
                (kernel_wide * spectrum).astype(jnp.bfloat16),
                (kernel_wide * spectrum_grad).astype(jnp.bfloat16),
            ],
            axis=1,
        )
        back = lax.dot_general(
            factor, domain, (((0,), (0,)), ((), ())), preferred_element_type=jnp.float32
        )
        for half in range(2):
            scattered[half, pl.ds(k, order, stride=rows), :] = back[:, halves[half]]
        return carry

    def several(g, carry):
        for n in range(UNROLL):
            step(g * UNROLL + n, carry)
        return carry

    lax.fori_loop(0, rows // UNROLL, several, 0)

    for n, block_ref in enumerate(sends):
        where = span(n % ranks, n // ranks, sent_parts)
        for half in range(2):
            block = scattered[half, where, :].astype(jnp.bfloat16)
            block_ref[:, :, halves[half]] = block.reshape(share // sent_parts, rows, width)


def gate_kernel(*refs):
    pass


def left_back_kernel(ranks, terms, rank_ref, values_ref, cotangent_ref, left_ref, *refs):
    moves = moves_of(ranks)
    arrived, reduced = refs[:ranks], refs[ranks : ranks + terms]
    mixed_ref, values_grad_ref, kernel_grad_ref, token_ref = refs[-4:]
    token_ref[...] = jnp.zeros_like(token_ref)
    blocks, order, _ = left_ref.shape
    share = order // ranks
    width = values_ref.shape[2]
    rank = rank_ref[0]
    for i in range(blocks):
        rows = slice(i * order, (i + 1) * order)
        factor = jnp.concatenate(
            [left_ref[i, pl.ds(pl.multiple_of((rank ^ m) * share, share), share), :] for m in moves],
            axis=0,
        )
        back = jnp.concatenate([arrived[m][i] for m in range(ranks)], axis=0)
        result = lax.dot_general(
            factor, back, (((0,), (0,)), ((), ())), preferred_element_type=jnp.float32
        )
        convolved, carried = result[:, :width], result[:, width:]
        source = values_ref[0, rows, :].astype(jnp.float32)
        upstream = cotangent_ref[0, rows, :].astype(jnp.float32)
        mixed_ref[0, rows, :] = (source * convolved).astype(jnp.bfloat16)
        values_grad_ref[0, rows, :] = (upstream * convolved + carried).astype(jnp.bfloat16)
    for n in range(terms):
        lanes = reduced[n].shape[1]
        kernel_grad_ref[:, n * lanes : (n + 1) * lanes] = reduced[n][...].astype(jnp.float32)


def per_device(values, cotangent, kernel, left_factor, right_factor, ranks, groups):
    sequences, row_count, channels = values.shape
    local, order, _ = left_factor.shape
    width = WIDTH
    lanes = 2 * width
    blocks = min(4, local)
    rows = min(ROWS, local)
    chunks = channels // width
    moves = moves_of(ranks)
    rank = lax.axis_index("seq").astype(jnp.int32).reshape(1)
    params = pltpu.CompilerParams(vmem_limit_bytes=VMEM_LIMIT)
    there = {q: 2 if q == 0 else 1 for q in range(chunks)}
    back = {q: 2 if q == chunks - 1 else 1 for q in range(chunks)}

    def buffer(parts):
        return jax.ShapeDtypeStruct((local // parts, local, lanes), jnp.bfloat16)

    def field_spec(q, first=0):
        return pl.BlockSpec((1, blocks * order, width), lambda g, rank: (0, first + g, q))

    def factor_spec(size, first=0):
        return pl.BlockSpec((size, order, order), lambda g, rank: (first + g, 0, 0))

    token = jax.ShapeDtypeStruct(TOKEN, jnp.float32)
    token_spec = pl.BlockSpec(TOKEN, lambda g, rank: (0, 0))

    def unread(after):
        return [pl.BlockSpec(memory_space=pl.ANY)] * len(after)

    def left_forward(q, part, after):
        steps = local // blocks // there[q]
        first = part * steps
        return pl.pallas_call(
            functools.partial(left_forward_kernel, ranks),
            out_shape=[buffer(there[q])] * ranks + [token],
            grid_spec=pltpu.PrefetchScalarGridSpec(
                num_scalar_prefetch=1,
                grid=(steps,),
                in_specs=[field_spec(q, first), field_spec(q, first), factor_spec(blocks, first)]
                + unread(after),
                out_specs=[pl.BlockSpec((blocks, local, lanes), lambda g, rank: (g, 0, 0))] * ranks
                + [token_spec],
            ),
            compiler_params=params,
            cost_estimate=COST,
        )(rank, values, cotangent, left_factor, *after)

    def exchange(sends):
        return [sends[0]] + [
            lax.ppermute(sends[n], "seq", [(r, r ^ moves[n]) for r in range(ranks)])
            for n in range(1, ranks)
        ]

    def right_both(q, arrived, terms, after):
        held = [] if terms is None else [terms]
        ins, outs = there[q], back[q]

        def moved(parts):
            spec = pl.BlockSpec((local // parts, rows, lanes), lambda g, rank: (0, g, 0))
            return [spec] * (parts * ranks)

        return pl.pallas_call(
            functools.partial(right_kernel, ranks, ins, outs),
            out_shape=[buffer(outs)] * (outs * ranks)
            + [jax.ShapeDtypeStruct((row_count, channels), jnp.bfloat16), token],
            grid_spec=pltpu.PrefetchScalarGridSpec(
                num_scalar_prefetch=1,
                grid=(local // rows,),
                in_specs=[
                    pl.BlockSpec((rows * order, width), lambda g, rank: (g, q)),
                    factor_spec(rows),
                ]
                + moved(ins)
                + unread(held)
                + unread(after),
                out_specs=moved(outs)
                + [pl.BlockSpec((rows * order, width), lambda g, rank: (g, q)), token_spec],
                scratch_shapes=[
                    pltpu.VMEM((2, order * rows, width), jnp.float32),
                    pltpu.VMEM((2, order * rows, width), jnp.float32),
                ],
            ),
            input_output_aliases={3 + ins * ranks: outs * ranks} if held else {},
            compiler_params=params,
            cost_estimate=COST,
        )(rank, kernel, right_factor, *arrived, *held, *after)

    def gate(held, after):
        return list(
            pl.pallas_call(
                gate_kernel,
                out_shape=[jax.ShapeDtypeStruct(x.shape, x.dtype) for x in held],
                in_specs=unread(held) + unread(after),
                out_specs=unread(held),
                input_output_aliases={n: n for n in range(len(held))},
                compiler_params=params,
                cost_estimate=COST,
            )(*held, *after)
        )

    def left_back(q, part, arrived, reduced, outputs, after):
        steps = local // blocks // back[q]
        first = part * steps
        shard = row_count // groups
        out_shape = [
            jax.ShapeDtypeStruct(values.shape, jnp.bfloat16),
            jax.ShapeDtypeStruct(values.shape, jnp.bfloat16),
            jax.ShapeDtypeStruct((shard, channels), jnp.float32),
            token,
        ]
        earlier = list(outputs) if outputs else []
        terms = len(reduced)
        aliases = {4 + ranks + terms + n: n for n in range(len(earlier))}
        grad_spec = pl.BlockSpec((shard * blocks // local, channels), lambda g, rank: (first + g, 0))
        return pl.pallas_call(
            functools.partial(left_back_kernel, ranks, terms),
            out_shape=out_shape,
            grid_spec=pltpu.PrefetchScalarGridSpec(
                num_scalar_prefetch=1,
                grid=(steps,),
                in_specs=[
                    field_spec(q, first),
                    field_spec(q, first),
                    factor_spec(blocks, first),
                ]
                + [pl.BlockSpec((blocks, local, lanes), lambda g, rank: (g, 0, 0))] * ranks
                + [grad_spec] * terms
                + unread(earlier)
                + unread(after),
                out_specs=[
                    field_spec(q, first),
                    field_spec(q, first),
                    grad_spec if terms else pl.BlockSpec(memory_space=pl.ANY),
                    token_spec,
                ],
            ),
            input_output_aliases=aliases,
            compiler_params=params,
            cost_estimate=COST,
        )(rank, values, cotangent, left_factor, *arrived, *reduced, *earlier, *after)

    received, sent, returned = {}, {}, {}
    left_tokens, right_tokens, back_tokens = [], {}, {}
    terms, outputs = None, []

    parts = {}
    for q in range(chunks):
        parts[q] = []
        for part in range(there[q]):
            *sends, done = left_forward(q, part, left_tokens[-1:])
            left_tokens.append(done)
            parts[q].append(sends)

    def send_left(q):
        received[q] = []
        for sends in parts[q]:
            if q == 1:
                sends[1 + FIRST :] = gate(sends[1 + FIRST :], left_tokens[-1:])
            if q >= 2:
                sends[1 + EARLY :] = gate(sends[1 + EARLY :], [right_tokens[q - 2]])
            received[q] += exchange(sends)

    for q in range(min(2, chunks)):
        send_left(q)
    for q in range(chunks):
        after = [right_tokens[q - 1]] if q else []
        *sent[q], terms, right_tokens[q] = right_both(q, received[q], terms, after)
        if q + 2 < chunks:
            send_left(q + 2)

    def back_step(q):
        last = [reduced] if q == chunks - 1 else []
        for part in range(back[q]):
            arrived = returned[q][part * ranks : (part + 1) * ranks]
            after = [right_tokens[chunks - 1]]
            *outputs[:], back_tokens[q] = left_back(q, part, arrived, last, outputs, after)

    for q in range(chunks):
        returned[q] = []
        for part in range(back[q]):
            sends = list(sent[q][part * ranks : (part + 1) * ranks])
            after = []
            if 1 <= q < chunks - 1:
                after.append(right_tokens[chunks - 1])
            if q >= 2:
                after.append(back_tokens[q - 2 + part])
            if q == 0 and chunks > 2:
                sends[1 : 1 + EARLY] = gate(sends[1 : 1 + EARLY], [right_tokens[chunks - 2]])
            if after:
                sends[1:] = gate(sends[1:], after)
            returned[q] += exchange(sends)
            if q >= 1 and part == 0:
                back_step(q - 1)
        if q == 0:
            (terms,) = gate([terms], returned[0][1 : 1 + EARLY])
            reduced = lax.psum_scatter(terms, "dp", scatter_dimension=0, tiled=True)
    back_step(chunks - 1)
    return tuple(outputs)


def solution(mesh):
    in_specs = (
        P("dp", "seq", None),
        P("dp", "seq", None),
        P("seq", None),
        P("seq", None, None),
        P("seq", None, None),
    )
    out_specs = (P("dp", "seq", None), P("dp", "seq", None), P(("seq", "dp"), None))
    return jax.shard_map(
        functools.partial(per_device, ranks=mesh.shape["seq"], groups=mesh.shape["dp"]),
        mesh=mesh,
        in_specs=in_specs,
        out_specs=out_specs,
        check_vma=False,
    )
```

```python
import functools

import jax
import jax.numpy as jnp
from jax import lax
from jax.experimental import pallas as pl
from jax.experimental.pallas import tpu as pltpu
from jax.sharding import PartitionSpec as P

WIDTH = 128
ROWS = 16
VMEM_LIMIT = 60 * 1024 * 1024
COST = pl.CostEstimate(flops=1024, bytes_accessed=1024, transcendentals=0)
FIRST = 5
EARLY = 3
UNROLL = 8
TOKEN = (8, 128)


def moves_of(ranks):
    far, near = list(range(ranks - 2, ranks)), list(range(2, ranks - 2))
    return [0, far[0]] + near[::2] + [far[1]] + near[1::2] + [1]


def left_forward_kernel(ranks, rank_ref, values_ref, cotangent_ref, left_ref, *refs):
    moves = moves_of(ranks)
    *sends, token_ref = refs[-ranks - 1 :]
    token_ref[...] = jnp.zeros_like(token_ref)
    blocks, order, _ = left_ref.shape
    share = order // ranks
    rank = rank_ref[0]
    for i in range(blocks):
        rows = slice(i * order, (i + 1) * order)
        source = values_ref[0, rows, :]
        gated = source.astype(jnp.float32) * cotangent_ref[0, rows, :].astype(jnp.float32)
        both = jnp.concatenate([source, gated.astype(jnp.bfloat16)], axis=1)
        factor = jnp.concatenate(
            [left_ref[i, pl.ds(pl.multiple_of((rank ^ m) * share, share), share), :] for m in moves],
            axis=0,
        )
        first = jnp.dot(factor, both, preferred_element_type=jnp.float32).astype(jnp.bfloat16)
        for m in range(ranks):
            sends[m][i] = first[m * share : (m + 1) * share]


def right_kernel(ranks, arrived_parts, sent_parts, rank_ref, kernel_ref, right_ref, *refs):
    arrived = refs[: arrived_parts * ranks]
    *sends, term_ref, token_ref, gathered, scattered = refs[-sent_parts * ranks - 4 :]
    token_ref[...] = jnp.zeros_like(token_ref)
    _, rows, lanes = arrived[0].shape
    order = right_ref.shape[1]
    share = order // ranks
    width = lanes // 2
    rank = rank_ref[0]
    halves = [slice(0, width), slice(width, lanes)]

    moves = moves_of(ranks)

    def span(n, part, parts):
        size = share * rows // parts
        start = (rank ^ moves[n]) * (share * rows) + part * size
        return pl.ds(pl.multiple_of(start, size), size)

    for n, block_ref in enumerate(arrived):
        where = span(n % ranks, n // ranks, arrived_parts)
        for half in range(2):
            block = block_ref[:, :, halves[half]].astype(jnp.float32)
            gathered[half, where, :] = block.reshape(where.size, width)

    def step(k, carry):
        both = jnp.concatenate(
            [gathered[half, pl.ds(k, order, stride=rows), :] for half in range(2)], axis=1
        ).astype(jnp.bfloat16)
        factor = right_ref[k]
        result = jnp.dot(factor, both, preferred_element_type=jnp.float32)
        spectrum = result[:, :width].astype(jnp.bfloat16).astype(jnp.float32)
        spectrum_grad = result[:, width:]
        here = pl.ds(pl.multiple_of(k * order, order), order)
        kernel_wide = kernel_ref[here, :].astype(jnp.float32)
        term_ref[here, :] = (spectrum_grad * spectrum).astype(jnp.bfloat16)
        domain = jnp.concatenate(
            [
                (kernel_wide * spectrum).astype(jnp.bfloat16),
                (kernel_wide * spectrum_grad).astype(jnp.bfloat16),
            ],
            axis=1,
        )
        back = lax.dot_general(
            factor, domain, (((0,), (0,)), ((), ())), preferred_element_type=jnp.float32
        )
        for half in range(2):
            scattered[half, pl.ds(k, order, stride=rows), :] = back[:, halves[half]]
        return carry

    def several(g, carry):
        for n in range(UNROLL):
            step(g * UNROLL + n, carry)
        return carry

    lax.fori_loop(0, rows // UNROLL, several, 0)

    for n, block_ref in enumerate(sends):
        where = span(n % ranks, n // ranks, sent_parts)
        for half in range(2):
            block = scattered[half, where, :].astype(jnp.bfloat16)
            block_ref[:, :, halves[half]] = block.reshape(share // sent_parts, rows, width)


def gate_kernel(*refs):
    pass


def left_back_kernel(ranks, terms, rank_ref, values_ref, cotangent_ref, left_ref, *refs):
    moves = moves_of(ranks)
    arrived, reduced = refs[:ranks], refs[ranks : ranks + terms]
    mixed_ref, values_grad_ref, kernel_grad_ref, token_ref = refs[-4:]
    token_ref[...] = jnp.zeros_like(token_ref)
    blocks, order, _ = left_ref.shape
    share = order // ranks
    width = values_ref.shape[2]
    rank = rank_ref[0]
    for i in range(blocks):
        rows = slice(i * order, (i + 1) * order)
        factor = jnp.concatenate(
            [left_ref[i, pl.ds(pl.multiple_of((rank ^ m) * share, share), share), :] for m in moves],
            axis=0,
        )
        back = jnp.concatenate([arrived[m][i] for m in range(ranks)], axis=0)
        result = lax.dot_general(
            factor, back, (((0,), (0,)), ((), ())), preferred_element_type=jnp.float32
        )
        convolved, carried = result[:, :width], result[:, width:]
        source = values_ref[0, rows, :].astype(jnp.float32)
        upstream = cotangent_ref[0, rows, :].astype(jnp.float32)
        mixed_ref[0, rows, :] = (source * convolved).astype(jnp.bfloat16)
        values_grad_ref[0, rows, :] = (upstream * convolved + carried).astype(jnp.bfloat16)
    for n in range(terms):
        lanes = reduced[n].shape[1]
        kernel_grad_ref[:, n * lanes : (n + 1) * lanes] = reduced[n][...].astype(jnp.float32)


def per_device(values, cotangent, kernel, left_factor, right_factor, ranks, groups):
    sequences, row_count, channels = values.shape
    local, order, _ = left_factor.shape
    width = WIDTH
    lanes = 2 * width
    blocks = min(8, local // 2)
    rows = min(ROWS, local)
    chunks = channels // width
    moves = moves_of(ranks)
    rank = lax.axis_index("seq").astype(jnp.int32).reshape(1)
    params = pltpu.CompilerParams(vmem_limit_bytes=VMEM_LIMIT)
    there = {q: 2 if q == 0 else 1 for q in range(chunks)}
    back = {q: 2 if q == chunks - 1 else 1 for q in range(chunks)}

    def buffer(parts):
        return jax.ShapeDtypeStruct((local // parts, local, lanes), jnp.bfloat16)

    def field_spec(q, first=0):
        return pl.BlockSpec((1, blocks * order, width), lambda g, rank: (0, first + g, q))

    def factor_spec(size, first=0):
        return pl.BlockSpec((size, order, order), lambda g, rank: (first + g, 0, 0))

    token = jax.ShapeDtypeStruct(TOKEN, jnp.float32)
    token_spec = pl.BlockSpec(TOKEN, lambda g, rank: (0, 0))

    def unread(after):
        return [pl.BlockSpec(memory_space=pl.ANY)] * len(after)

    def left_forward(q, part, after):
        steps = local // blocks // there[q]
        first = part * steps
        return pl.pallas_call(
            functools.partial(left_forward_kernel, ranks),
            out_shape=[buffer(there[q])] * ranks + [token],
            grid_spec=pltpu.PrefetchScalarGridSpec(
                num_scalar_prefetch=1,
                grid=(steps,),
                in_specs=[field_spec(q, first), field_spec(q, first), factor_spec(blocks, first)]
                + unread(after),
                out_specs=[pl.BlockSpec((blocks, local, lanes), lambda g, rank: (g, 0, 0))] * ranks
                + [token_spec],
            ),
            compiler_params=params,
            cost_estimate=COST,
        )(rank, values, cotangent, left_factor, *after)

    def exchange(sends):
        return [sends[0]] + [
            lax.ppermute(sends[n], "seq", [(r, r ^ moves[n]) for r in range(ranks)])
            for n in range(1, ranks)
        ]

    def right_both(q, arrived, terms, after):
        held = [] if terms is None else [terms]
        ins, outs = there[q], back[q]

        def moved(parts):
            spec = pl.BlockSpec((local // parts, rows, lanes), lambda g, rank: (0, g, 0))
            return [spec] * (parts * ranks)

        return pl.pallas_call(
            functools.partial(right_kernel, ranks, ins, outs),
            out_shape=[buffer(outs)] * (outs * ranks)
            + [jax.ShapeDtypeStruct((row_count, channels), jnp.bfloat16), token],
            grid_spec=pltpu.PrefetchScalarGridSpec(
                num_scalar_prefetch=1,
                grid=(local // rows,),
                in_specs=[
                    pl.BlockSpec((rows * order, width), lambda g, rank: (g, q)),
                    factor_spec(rows),
                ]
                + moved(ins)
                + unread(held)
                + unread(after),
                out_specs=moved(outs)
                + [pl.BlockSpec((rows * order, width), lambda g, rank: (g, q)), token_spec],
                scratch_shapes=[
                    pltpu.VMEM((2, order * rows, width), jnp.float32),
                    pltpu.VMEM((2, order * rows, width), jnp.float32),
                ],
            ),
            input_output_aliases={3 + ins * ranks: outs * ranks} if held else {},
            compiler_params=params,
            cost_estimate=COST,
        )(rank, kernel, right_factor, *arrived, *held, *after)

    def gate(held, after):
        return list(
            pl.pallas_call(
                gate_kernel,
                out_shape=[jax.ShapeDtypeStruct(x.shape, x.dtype) for x in held],
                in_specs=unread(held) + unread(after),
                out_specs=unread(held),
                input_output_aliases={n: n for n in range(len(held))},
                compiler_params=params,
                cost_estimate=COST,
            )(*held, *after)
        )

    def left_back(q, part, arrived, reduced, outputs, after):
        steps = local // blocks // back[q]
        first = part * steps
        shard = row_count // groups
        out_shape = [
            jax.ShapeDtypeStruct(values.shape, jnp.bfloat16),
            jax.ShapeDtypeStruct(values.shape, jnp.bfloat16),
            jax.ShapeDtypeStruct((shard, channels), jnp.float32),
            token,
        ]
        earlier = list(outputs) if outputs else []
        terms = len(reduced)
        aliases = {4 + ranks + terms + n: n for n in range(len(earlier))}
        grad_spec = pl.BlockSpec((shard // steps, channels), lambda g, rank: (g, 0))
        return pl.pallas_call(
            functools.partial(left_back_kernel, ranks, terms),
            out_shape=out_shape,
            grid_spec=pltpu.PrefetchScalarGridSpec(
                num_scalar_prefetch=1,
                grid=(steps,),
                in_specs=[
                    field_spec(q, first),
                    field_spec(q, first),
                    factor_spec(blocks, first),
                ]
                + [pl.BlockSpec((blocks, local, lanes), lambda g, rank: (g, 0, 0))] * ranks
                + [grad_spec] * terms
                + unread(earlier)
                + unread(after),
                out_specs=[
                    field_spec(q, first),
                    field_spec(q, first),
                    grad_spec if terms else pl.BlockSpec(memory_space=pl.ANY),
                    token_spec,
                ],
            ),
            input_output_aliases=aliases,
            compiler_params=params,
            cost_estimate=COST,
        )(rank, values, cotangent, left_factor, *arrived, *reduced, *earlier, *after)

    received, sent, returned = {}, {}, {}
    left_tokens, right_tokens, back_tokens = [], {}, {}
    terms, outputs = None, []

    parts = {}
    for q in range(chunks):
        parts[q] = []
        for part in range(there[q]):
            *sends, done = left_forward(q, part, left_tokens[-1:])
            left_tokens.append(done)
            parts[q].append(sends)

    def send_left(q):
        received[q] = []
        for sends in parts[q]:
            if q == 1:
                sends[1 + FIRST :] = gate(sends[1 + FIRST :], left_tokens[-1:])
            if q >= 2:
                sends[1 + EARLY :] = gate(sends[1 + EARLY :], [right_tokens[q - 2]])
            received[q] += exchange(sends)

    for q in range(min(2, chunks)):
        send_left(q)
    for q in range(chunks):
        after = [right_tokens[q - 1]] if q else []
        *sent[q], terms, right_tokens[q] = right_both(q, received[q], terms, after)
        if q + 2 < chunks:
            send_left(q + 2)

    def back_step(q):
        last = [reduced] if q == chunks - 1 else []
        for part in range(back[q]):
            arrived = returned[q][part * ranks : (part + 1) * ranks]
            after = [right_tokens[chunks - 1]]
            *outputs[:], back_tokens[q] = left_back(q, part, arrived, last, outputs, after)
            last = []

    for q in range(chunks):
        returned[q] = []
        for part in range(back[q]):
            sends = list(sent[q][part * ranks : (part + 1) * ranks])
            after = []
            if 1 <= q < chunks - 1:
                after.append(right_tokens[chunks - 1])
            if q >= 2:
                after.append(back_tokens[q - 2 + part])
            if q == 0 and chunks > 2:
                sends[1 : 1 + EARLY] = gate(sends[1 : 1 + EARLY], [right_tokens[chunks - 2]])
            if after:
                sends[1:] = gate(sends[1:], after)
            returned[q] += exchange(sends)
            if q >= 1 and part == 0:
                back_step(q - 1)
        if q == 0:
            (terms,) = gate([terms], returned[0][1 : 1 + EARLY])
            reduced = lax.psum_scatter(terms, "dp", scatter_dimension=0, tiled=True)
    back_step(chunks - 1)
    return tuple(outputs)


def solution(mesh):
    in_specs = (
        P("dp", "seq", None),
        P("dp", "seq", None),
        P("seq", None),
        P("seq", None, None),
        P("seq", None, None),
    )
    out_specs = (P("dp", "seq", None), P("dp", "seq", None), P(("seq", "dp"), None))
    return jax.shard_map(
        functools.partial(per_device, ranks=mesh.shape["seq"], groups=mesh.shape["dp"]),
        mesh=mesh,
        in_specs=in_specs,
        out_specs=out_specs,
        check_vma=False,
    )
```

```python
import functools

import jax
import jax.numpy as jnp
from jax import lax
from jax.experimental import pallas as pl
from jax.experimental.pallas import tpu as pltpu
from jax.sharding import PartitionSpec as P

WIDTH = 128
ROWS = 16
VMEM_LIMIT = 60 * 1024 * 1024
COST = pl.CostEstimate(flops=1024, bytes_accessed=1024, transcendentals=0)
FIRST = 5
EARLY = 3
UNROLL = 8
TOKEN = (8, 128)


def moves_of(ranks):
    far, near = list(range(ranks - 2, ranks)), list(range(2, ranks - 2))
    return [0, far[0]] + near[::2] + [far[1]] + near[1::2] + [1]


def left_forward_kernel(ranks, rank_ref, values_ref, cotangent_ref, left_ref, *refs):
    moves = moves_of(ranks)
    *sends, token_ref = refs[-ranks - 1 :]
    token_ref[...] = jnp.zeros_like(token_ref)
    blocks, order, _ = left_ref.shape
    share = order // ranks
    rank = rank_ref[0]
    for i in range(blocks):
        rows = slice(i * order, (i + 1) * order)
        source = values_ref[0, rows, :]
        gated = source.astype(jnp.float32) * cotangent_ref[0, rows, :].astype(jnp.float32)
        both = jnp.concatenate([source, gated.astype(jnp.bfloat16)], axis=1)
        factor = jnp.concatenate(
            [left_ref[i, pl.ds(pl.multiple_of((rank ^ m) * share, share), share), :] for m in moves],
            axis=0,
        )
        first = jnp.dot(factor, both, preferred_element_type=jnp.float32).astype(jnp.bfloat16)
        for m in range(ranks):
            sends[m][i] = first[m * share : (m + 1) * share]


def right_kernel(ranks, arrived_parts, sent_parts, rank_ref, kernel_ref, right_ref, *refs):
    arrived = refs[: arrived_parts * ranks]
    *sends, term_ref, token_ref, gathered, scattered = refs[-sent_parts * ranks - 4 :]
    token_ref[...] = jnp.zeros_like(token_ref)
    _, rows, lanes = arrived[0].shape
    order = right_ref.shape[1]
    share = order // ranks
    width = lanes // 2
    rank = rank_ref[0]
    halves = [slice(0, width), slice(width, lanes)]

    moves = moves_of(ranks)

    def span(n, part, parts):
        size = share * rows // parts
        start = (rank ^ moves[n]) * (share * rows) + part * size
        return pl.ds(pl.multiple_of(start, size), size)

    for n, block_ref in enumerate(arrived):
        where = span(n % ranks, n // ranks, arrived_parts)
        for half in range(2):
            block = block_ref[:, :, halves[half]].astype(jnp.float32)
            gathered[half, where, :] = block.reshape(where.size, width)

    def step(k, carry):
        both = jnp.concatenate(
            [gathered[half, pl.ds(k, order, stride=rows), :] for half in range(2)], axis=1
        ).astype(jnp.bfloat16)
        factor = right_ref[k]
        result = jnp.dot(factor, both, preferred_element_type=jnp.float32)
        spectrum = result[:, :width].astype(jnp.bfloat16).astype(jnp.float32)
        spectrum_grad = result[:, width:]
        here = pl.ds(pl.multiple_of(k * order, order), order)
        kernel_wide = kernel_ref[here, :].astype(jnp.float32)
        term_ref[here, :] = (spectrum_grad * spectrum).astype(jnp.bfloat16)
        domain = jnp.concatenate(
            [
                (kernel_wide * spectrum).astype(jnp.bfloat16),
                (kernel_wide * spectrum_grad).astype(jnp.bfloat16),
            ],
            axis=1,
        )
        back = lax.dot_general(
            factor, domain, (((0,), (0,)), ((), ())), preferred_element_type=jnp.float32
        )
        for half in range(2):
            scattered[half, pl.ds(k, order, stride=rows), :] = back[:, halves[half]]
        return carry

    def several(g, carry):
        for n in range(UNROLL):
            step(g * UNROLL + n, carry)
        return carry

    lax.fori_loop(0, rows // UNROLL, several, 0)

    for n, block_ref in enumerate(sends):
        where = span(n % ranks, n // ranks, sent_parts)
        for half in range(2):
            block = scattered[half, where, :].astype(jnp.bfloat16)
            block_ref[:, :, halves[half]] = block.reshape(share // sent_parts, rows, width)


def gate_kernel(*refs):
    pass


def left_back_kernel(ranks, terms, rank_ref, values_ref, cotangent_ref, left_ref, *refs):
    moves = moves_of(ranks)
    arrived, reduced = refs[:ranks], refs[ranks : ranks + terms]
    mixed_ref, values_grad_ref, kernel_grad_ref, token_ref = refs[-4:]
    token_ref[...] = jnp.zeros_like(token_ref)
    blocks, order, _ = left_ref.shape
    share = order // ranks
    width = values_ref.shape[2]
    rank = rank_ref[0]
    for i in range(blocks):
        rows = slice(i * order, (i + 1) * order)
        factor = jnp.concatenate(
            [left_ref[i, pl.ds(pl.multiple_of((rank ^ m) * share, share), share), :] for m in moves],
            axis=0,
        )
        back = jnp.concatenate([arrived[m][i] for m in range(ranks)], axis=0)
        result = lax.dot_general(
            factor, back, (((0,), (0,)), ((), ())), preferred_element_type=jnp.float32
        )
        convolved, carried = result[:, :width], result[:, width:]
        source = values_ref[0, rows, :].astype(jnp.float32)
        upstream = cotangent_ref[0, rows, :].astype(jnp.float32)
        mixed_ref[0, rows, :] = (source * convolved).astype(jnp.bfloat16)
        values_grad_ref[0, rows, :] = (upstream * convolved + carried).astype(jnp.bfloat16)
    for n in range(terms):
        lanes = reduced[n].shape[1]
        kernel_grad_ref[:, n * lanes : (n + 1) * lanes] = reduced[n][...].astype(jnp.float32)


def per_device(values, cotangent, kernel, left_factor, right_factor, ranks, groups):
    sequences, row_count, channels = values.shape
    local, order, _ = left_factor.shape
    width = WIDTH
    lanes = 2 * width
    blocks = min(8, local // 2)
    rows = min(ROWS, local)
    chunks = channels // width
    moves = moves_of(ranks)
    rank = lax.axis_index("seq").astype(jnp.int32).reshape(1)
    params = pltpu.CompilerParams(vmem_limit_bytes=VMEM_LIMIT)
    there = {q: 2 if q == 0 else 1 for q in range(chunks)}
    back = {q: 2 if q == chunks - 1 else 1 for q in range(chunks)}

    def buffer(parts):
        return jax.ShapeDtypeStruct((local // parts, local, lanes), jnp.bfloat16)

    def field_spec(q, first=0):
        return pl.BlockSpec((1, blocks * order, width), lambda g, rank: (0, first + g, q))

    def factor_spec(size, first=0):
        return pl.BlockSpec((size, order, order), lambda g, rank: (first + g, 0, 0))

    token = jax.ShapeDtypeStruct(TOKEN, jnp.float32)
    token_spec = pl.BlockSpec(TOKEN, lambda g, rank: (0, 0))

    def unread(after):
        return [pl.BlockSpec(memory_space=pl.ANY)] * len(after)

    def left_forward(q, part, after):
        steps = local // blocks // there[q]
        first = part * steps
        return pl.pallas_call(
            functools.partial(left_forward_kernel, ranks),
            out_shape=[buffer(there[q])] * ranks + [token],
            grid_spec=pltpu.PrefetchScalarGridSpec(
                num_scalar_prefetch=1,
                grid=(steps,),
                in_specs=[field_spec(q, first), field_spec(q, first), factor_spec(blocks, first)]
                + unread(after),
                out_specs=[pl.BlockSpec((blocks, local, lanes), lambda g, rank: (g, 0, 0))] * ranks
                + [token_spec],
            ),
            compiler_params=params,
            cost_estimate=COST,
        )(rank, values, cotangent, left_factor, *after)

    def exchange(sends):
        return [sends[0]] + [
            lax.ppermute(sends[n], "seq", [(r, r ^ moves[n]) for r in range(ranks)])
            for n in range(1, ranks)
        ]

    def right_both(q, arrived, terms, after):
        held = [] if terms is None else [terms]
        ins, outs = there[q], back[q]

        def moved(parts):
            spec = pl.BlockSpec((local // parts, rows, lanes), lambda g, rank: (0, g, 0))
            return [spec] * (parts * ranks)

        return pl.pallas_call(
            functools.partial(right_kernel, ranks, ins, outs),
            out_shape=[buffer(outs)] * (outs * ranks)
            + [jax.ShapeDtypeStruct((row_count, channels), jnp.bfloat16), token],
            grid_spec=pltpu.PrefetchScalarGridSpec(
                num_scalar_prefetch=1,
                grid=(local // rows,),
                in_specs=[
                    pl.BlockSpec((rows * order, width), lambda g, rank: (g, q)),
                    factor_spec(rows),
                ]
                + moved(ins)
                + unread(held)
                + unread(after),
                out_specs=moved(outs)
                + [pl.BlockSpec((rows * order, width), lambda g, rank: (g, q)), token_spec],
                scratch_shapes=[
                    pltpu.VMEM((2, order * rows, width), jnp.float32),
                    pltpu.VMEM((2, order * rows, width), jnp.float32),
                ],
            ),
            input_output_aliases={3 + ins * ranks: outs * ranks} if held else {},
            compiler_params=params,
            cost_estimate=COST,
        )(rank, kernel, right_factor, *arrived, *held, *after)

    def gate(held, after, limit=VMEM_LIMIT):
        return list(
            pl.pallas_call(
                gate_kernel,
                out_shape=[jax.ShapeDtypeStruct(x.shape, x.dtype) for x in held],
                in_specs=unread(held) + unread(after),
                out_specs=unread(held),
                input_output_aliases={n: n for n in range(len(held))},
                compiler_params=pltpu.CompilerParams(vmem_limit_bytes=limit),
                cost_estimate=COST,
            )(*held, *after)
        )

    def left_back(q, part, arrived, reduced, outputs, after):
        steps = local // blocks // back[q]
        first = part * steps
        shard = row_count // groups
        out_shape = [
            jax.ShapeDtypeStruct(values.shape, jnp.bfloat16),
            jax.ShapeDtypeStruct(values.shape, jnp.bfloat16),
            jax.ShapeDtypeStruct((shard, channels), jnp.float32),
            token,
        ]
        earlier = list(outputs) if outputs else []
        terms = len(reduced)
        aliases = {4 + ranks + terms + n: n for n in range(len(earlier))}
        grad_spec = pl.BlockSpec((shard // steps, channels), lambda g, rank: (g, 0))
        return pl.pallas_call(
            functools.partial(left_back_kernel, ranks, terms),
            out_shape=out_shape,
            grid_spec=pltpu.PrefetchScalarGridSpec(
                num_scalar_prefetch=1,
                grid=(steps,),
                in_specs=[
                    field_spec(q, first),
                    field_spec(q, first),
                    factor_spec(blocks, first),
                ]
                + [pl.BlockSpec((blocks, local, lanes), lambda g, rank: (g, 0, 0))] * ranks
                + [grad_spec] * terms
                + unread(earlier)
                + unread(after),
                out_specs=[
                    field_spec(q, first),
                    field_spec(q, first),
                    grad_spec if terms else pl.BlockSpec(memory_space=pl.ANY),
                    token_spec,
                ],
            ),
            input_output_aliases=aliases,
            compiler_params=pltpu.CompilerParams(vmem_limit_bytes=48 * 1024 * 1024),
            cost_estimate=COST,
        )(rank, values, cotangent, left_factor, *arrived, *reduced, *earlier, *after)

    received, sent, returned = {}, {}, {}
    left_tokens, right_tokens, back_tokens = [], {}, {}
    terms, outputs = None, []

    parts = {}
    for q in range(chunks):
        parts[q] = []
        for part in range(there[q]):
            *sends, done = left_forward(q, part, left_tokens[-1:])
            left_tokens.append(done)
            parts[q].append(sends)

    def send_left(q):
        received[q] = []
        for sends in parts[q]:
            if q == 1:
                sends[1 + FIRST :] = gate(sends[1 + FIRST :], left_tokens[-1:])
            if q >= 2:
                sends[1 + EARLY :] = gate(sends[1 + EARLY :], [right_tokens[q - 2]])
            received[q] += exchange(sends)

    for q in range(min(2, chunks)):
        send_left(q)
    for q in range(chunks):
        after = [right_tokens[q - 1]] if q else []
        *sent[q], terms, right_tokens[q] = right_both(q, received[q], terms, after)
        if q + 2 < chunks:
            send_left(q + 2)

    def back_step(q):
        last = [reduced] if q == chunks - 1 else []
        for part in range(back[q]):
            arrived = returned[q][part * ranks : (part + 1) * ranks]
            after = [right_tokens[chunks - 1]]
            *outputs[:], back_tokens[q] = left_back(q, part, arrived, last, outputs, after)
            last = []

    for q in range(chunks):
        returned[q] = []
        for part in range(back[q]):
            sends = list(sent[q][part * ranks : (part + 1) * ranks])
            after = []
            if 1 <= q < chunks - 1:
                after.append(right_tokens[chunks - 1])
            if q >= 2:
                after.append(back_tokens[q - 2 + part])
            if q == 0 and chunks > 2:
                sends[1 : 1 + EARLY] = gate(sends[1 : 1 + EARLY], [right_tokens[chunks - 2]])
            if after:
                sends[1:] = gate(sends[1:], after)
            returned[q] += exchange(sends)
            if q >= 1 and part == 0:
                back_step(q - 1)
        if q == 0:
            (terms,) = gate([terms], returned[0][1 : 1 + EARLY], 1 * 1024 * 1024)
            reduced = lax.psum_scatter(terms, "dp", scatter_dimension=0, tiled=True)
    back_step(chunks - 1)
    return tuple(outputs)


def solution(mesh):
    in_specs = (
        P("dp", "seq", None),
        P("dp", "seq", None),
        P("seq", None),
        P("seq", None, None),
        P("seq", None, None),
    )
    out_specs = (P("dp", "seq", None), P("dp", "seq", None), P(("seq", "dp"), None))
    return jax.shard_map(
        functools.partial(per_device, ranks=mesh.shape["seq"], groups=mesh.shape["dp"]),
        mesh=mesh,
        in_specs=in_specs,
        out_specs=out_specs,
        check_vma=False,
    )
```

```python
import functools

import jax
import jax.numpy as jnp
from jax import lax
from jax.experimental import pallas as pl
from jax.experimental.pallas import tpu as pltpu
from jax.sharding import PartitionSpec as P

WIDTH = 128
ROWS = 16
VMEM_LIMIT = 60 * 1024 * 1024
COST = pl.CostEstimate(flops=1024, bytes_accessed=1024, transcendentals=0)
FIRST = 5
EARLY = 3
UNROLL = 8
TOKEN = (8, 128)


def moves_of(ranks):
    far, near = list(range(ranks - 2, ranks)), list(range(2, ranks - 2))
    return [0, far[0]] + near[::2] + [far[1]] + near[1::2] + [1]


def left_forward_kernel(ranks, rank_ref, values_ref, cotangent_ref, left_ref, *refs):
    moves = moves_of(ranks)
    *sends, token_ref = refs[-ranks - 1 :]
    token_ref[...] = jnp.zeros_like(token_ref)
    blocks, order, _ = left_ref.shape
    share = order // ranks
    rank = rank_ref[0]
    for i in range(blocks):
        rows = slice(i * order, (i + 1) * order)
        source = values_ref[0, rows, :]
        gated = source.astype(jnp.float32) * cotangent_ref[0, rows, :].astype(jnp.float32)
        both = jnp.concatenate([source, gated.astype(jnp.bfloat16)], axis=1)
        factor = jnp.concatenate(
            [left_ref[i, pl.ds(pl.multiple_of((rank ^ m) * share, share), share), :] for m in moves],
            axis=0,
        )
        first = jnp.dot(factor, both, preferred_element_type=jnp.float32).astype(jnp.bfloat16)
        for m in range(ranks):
            sends[m][i] = first[m * share : (m + 1) * share]


def right_kernel(ranks, arrived_parts, sent_parts, rank_ref, kernel_ref, right_ref, *refs):
    arrived = refs[: arrived_parts * ranks]
    *sends, term_ref, token_ref, gathered, scattered = refs[-sent_parts * ranks - 4 :]
    token_ref[...] = jnp.zeros_like(token_ref)
    _, rows, lanes = arrived[0].shape
    order = right_ref.shape[1]
    share = order // ranks
    width = lanes // 2
    rank = rank_ref[0]
    halves = [slice(0, width), slice(width, lanes)]

    moves = moves_of(ranks)

    def span(n, part, parts):
        size = share * rows // parts
        start = (rank ^ moves[n]) * (share * rows) + part * size
        return pl.ds(pl.multiple_of(start, size), size)

    for n, block_ref in enumerate(arrived):
        where = span(n % ranks, n // ranks, arrived_parts)
        for half in range(2):
            block = block_ref[:, :, halves[half]].astype(jnp.float32)
            gathered[half, where, :] = block.reshape(where.size, width)

    def step(k, carry):
        both = jnp.concatenate(
            [gathered[half, pl.ds(k, order, stride=rows), :] for half in range(2)], axis=1
        ).astype(jnp.bfloat16)
        factor = right_ref[k]
        result = jnp.dot(factor, both, preferred_element_type=jnp.float32)
        spectrum = result[:, :width].astype(jnp.bfloat16).astype(jnp.float32)
        spectrum_grad = result[:, width:]
        here = pl.ds(pl.multiple_of(k * order, order), order)
        kernel_wide = kernel_ref[here, :].astype(jnp.float32)
        term_ref[here, :] = (spectrum_grad * spectrum).astype(jnp.bfloat16)
        domain = jnp.concatenate(
            [
                (kernel_wide * spectrum).astype(jnp.bfloat16),
                (kernel_wide * spectrum_grad).astype(jnp.bfloat16),
            ],
            axis=1,
        )
        back = lax.dot_general(
            factor, domain, (((0,), (0,)), ((), ())), preferred_element_type=jnp.float32
        )
        for half in range(2):
            scattered[half, pl.ds(k, order, stride=rows), :] = back[:, halves[half]]
        return carry

    def several(g, carry):
        for n in range(UNROLL):
            step(g * UNROLL + n, carry)
        return carry

    lax.fori_loop(0, rows // UNROLL, several, 0)

    for n, block_ref in enumerate(sends):
        where = span(n % ranks, n // ranks, sent_parts)
        for half in range(2):
            block = scattered[half, where, :].astype(jnp.bfloat16)
            block_ref[:, :, halves[half]] = block.reshape(share // sent_parts, rows, width)


def gate_kernel(*refs):
    pass


def left_back_kernel(ranks, terms, rank_ref, values_ref, cotangent_ref, left_ref, *refs):
    moves = moves_of(ranks)
    arrived, reduced = refs[:ranks], refs[ranks : ranks + terms]
    mixed_ref, values_grad_ref, kernel_grad_ref, token_ref = refs[-4:]
    token_ref[...] = jnp.zeros_like(token_ref)
    blocks, order, _ = left_ref.shape
    share = order // ranks
    width = values_ref.shape[2]
    rank = rank_ref[0]
    for i in range(blocks):
        rows = slice(i * order, (i + 1) * order)
        factor = jnp.concatenate(
            [left_ref[i, pl.ds(pl.multiple_of((rank ^ m) * share, share), share), :] for m in moves],
            axis=0,
        )
        back = jnp.concatenate([arrived[m][i] for m in range(ranks)], axis=0)
        result = lax.dot_general(
            factor, back, (((0,), (0,)), ((), ())), preferred_element_type=jnp.float32
        )
        convolved, carried = result[:, :width], result[:, width:]
        source = values_ref[0, rows, :].astype(jnp.float32)
        upstream = cotangent_ref[0, rows, :].astype(jnp.float32)
        mixed_ref[0, rows, :] = (source * convolved).astype(jnp.bfloat16)
        values_grad_ref[0, rows, :] = (upstream * convolved + carried).astype(jnp.bfloat16)
    for n in range(terms):
        lanes = reduced[n].shape[1]
        kernel_grad_ref[:, n * lanes : (n + 1) * lanes] = reduced[n][...].astype(jnp.float32)


def per_device(values, cotangent, kernel, left_factor, right_factor, ranks, groups):
    sequences, row_count, channels = values.shape
    local, order, _ = left_factor.shape
    width = WIDTH
    lanes = 2 * width
    blocks = min(8, local // 2)
    rows = min(ROWS, local)
    chunks = channels // width
    moves = moves_of(ranks)
    rank = lax.axis_index("seq").astype(jnp.int32).reshape(1)
    params = pltpu.CompilerParams(vmem_limit_bytes=VMEM_LIMIT)
    there = {q: 2 if q == 0 else 1 for q in range(chunks)}
    back = {q: 2 if q == chunks - 1 else 1 for q in range(chunks)}

    def buffer(parts):
        return jax.ShapeDtypeStruct((local // parts, local, lanes), jnp.bfloat16)

    def field_spec(q, first=0):
        return pl.BlockSpec((1, blocks * order, width), lambda g, rank: (0, first + g, q))

    def factor_spec(size, first=0):
        return pl.BlockSpec((size, order, order), lambda g, rank: (first + g, 0, 0))

    token = jax.ShapeDtypeStruct(TOKEN, jnp.float32)
    token_spec = pl.BlockSpec(TOKEN, lambda g, rank: (0, 0))

    def unread(after):
        return [pl.BlockSpec(memory_space=pl.ANY)] * len(after)

    def left_forward(q, part, after):
        steps = local // blocks // there[q]
        first = part * steps
        return pl.pallas_call(
            functools.partial(left_forward_kernel, ranks),
            out_shape=[buffer(there[q])] * ranks + [token],
            grid_spec=pltpu.PrefetchScalarGridSpec(
                num_scalar_prefetch=1,
                grid=(steps,),
                in_specs=[field_spec(q, first), field_spec(q, first), factor_spec(blocks, first)]
                + unread(after),
                out_specs=[pl.BlockSpec((blocks, local, lanes), lambda g, rank: (g, 0, 0))] * ranks
                + [token_spec],
            ),
            compiler_params=params,
            cost_estimate=COST,
        )(rank, values, cotangent, left_factor, *after)

    def exchange(sends):
        return [sends[0]] + [
            lax.ppermute(sends[n], "seq", [(r, r ^ moves[n]) for r in range(ranks)])
            for n in range(1, ranks)
        ]

    def right_both(q, arrived, terms, after):
        held = [] if terms is None else [terms]
        ins, outs = there[q], back[q]

        def moved(parts):
            spec = pl.BlockSpec((local // parts, rows, lanes), lambda g, rank: (0, g, 0))
            return [spec] * (parts * ranks)

        return pl.pallas_call(
            functools.partial(right_kernel, ranks, ins, outs),
            out_shape=[buffer(outs)] * (outs * ranks)
            + [jax.ShapeDtypeStruct((row_count, channels), jnp.bfloat16), token],
            grid_spec=pltpu.PrefetchScalarGridSpec(
                num_scalar_prefetch=1,
                grid=(local // rows,),
                in_specs=[
                    pl.BlockSpec((rows * order, width), lambda g, rank: (g, q)),
                    factor_spec(rows),
                ]
                + moved(ins)
                + unread(held)
                + unread(after),
                out_specs=moved(outs)
                + [pl.BlockSpec((rows * order, width), lambda g, rank: (g, q)), token_spec],
                scratch_shapes=[
                    pltpu.VMEM((2, order * rows, width), jnp.float32),
                    pltpu.VMEM((2, order * rows, width), jnp.float32),
                ],
            ),
            input_output_aliases={3 + ins * ranks: outs * ranks} if held else {},
            compiler_params=params,
            cost_estimate=COST,
        )(rank, kernel, right_factor, *arrived, *held, *after)

    def gate(held, after):
        return list(
            pl.pallas_call(
                gate_kernel,
                out_shape=[jax.ShapeDtypeStruct(x.shape, x.dtype) for x in held],
                in_specs=unread(held) + unread(after),
                out_specs=unread(held),
                input_output_aliases={n: n for n in range(len(held))},
                compiler_params=params,
                cost_estimate=COST,
            )(*held, *after)
        )

    def left_back(q, part, arrived, reduced, outputs, after):
        steps = local // blocks // back[q]
        first = part * steps
        shard = row_count // groups
        out_shape = [
            jax.ShapeDtypeStruct(values.shape, jnp.bfloat16),
            jax.ShapeDtypeStruct(values.shape, jnp.bfloat16),
            jax.ShapeDtypeStruct((shard, channels), jnp.float32),
            token,
        ]
        earlier = list(outputs) if outputs else []
        terms = len(reduced)
        aliases = {4 + ranks + terms + n: n for n in range(len(earlier))}
        grad_spec = pl.BlockSpec((shard // steps, channels), lambda g, rank: (g, 0))
        return pl.pallas_call(
            functools.partial(left_back_kernel, ranks, terms),
            out_shape=out_shape,
            grid_spec=pltpu.PrefetchScalarGridSpec(
                num_scalar_prefetch=1,
                grid=(steps,),
                in_specs=[
                    field_spec(q, first),
                    field_spec(q, first),
                    factor_spec(blocks, first),
                ]
                + [pl.BlockSpec((blocks, local, lanes), lambda g, rank: (g, 0, 0))] * ranks
                + [grad_spec] * terms
                + unread(earlier)
                + unread(after),
                out_specs=[
                    field_spec(q, first),
                    field_spec(q, first),
                    grad_spec if terms else pl.BlockSpec(memory_space=pl.ANY),
                    token_spec,
                ],
            ),
            input_output_aliases=aliases,
            compiler_params=pltpu.CompilerParams(vmem_limit_bytes=40 * 1024 * 1024),
            cost_estimate=COST,
        )(rank, values, cotangent, left_factor, *arrived, *reduced, *earlier, *after)

    received, sent, returned = {}, {}, {}
    left_tokens, right_tokens, back_tokens = [], {}, {}
    terms, outputs = None, []

    parts = {}
    for q in range(chunks):
        parts[q] = []
        for part in range(there[q]):
            *sends, done = left_forward(q, part, left_tokens[-1:])
            left_tokens.append(done)
            parts[q].append(sends)

    def send_left(q):
        received[q] = []
        for sends in parts[q]:
            if q == 1:
                sends[1 + FIRST :] = gate(sends[1 + FIRST :], left_tokens[-1:])
            if q >= 2:
                sends[1 + EARLY :] = gate(sends[1 + EARLY :], [right_tokens[q - 2]])
            received[q] += exchange(sends)

    for q in range(min(2, chunks)):
        send_left(q)
    for q in range(chunks):
        after = [right_tokens[q - 1]] if q else []
        *sent[q], terms, right_tokens[q] = right_both(q, received[q], terms, after)
        if q + 2 < chunks:
            send_left(q + 2)

    def back_step(q):
        last = [reduced] if q == chunks - 1 else []
        for part in range(back[q]):
            arrived = returned[q][part * ranks : (part + 1) * ranks]
            after = [right_tokens[chunks - 1]]
            *outputs[:], back_tokens[q] = left_back(q, part, arrived, last, outputs, after)
            last = []

    for q in range(chunks):
        returned[q] = []
        for part in range(back[q]):
            sends = list(sent[q][part * ranks : (part + 1) * ranks])
            after = []
            if 1 <= q < chunks - 1:
                after.append(right_tokens[chunks - 1])
            if q >= 2:
                after.append(back_tokens[q - 2 + part])
            if q == 0 and chunks > 2:
                sends[1 : 1 + EARLY] = gate(sends[1 : 1 + EARLY], [right_tokens[chunks - 2]])
            if after:
                sends[1:] = gate(sends[1:], after)
            returned[q] += exchange(sends)
            if q >= 1 and part == 0:
                back_step(q - 1)
        if q == 0:
            (terms,) = gate([terms], returned[0][1 : 1 + EARLY])
            reduced = lax.psum_scatter(terms, "dp", scatter_dimension=0, tiled=True)
    back_step(chunks - 1)
    return tuple(outputs)


def solution(mesh):
    in_specs = (
        P("dp", "seq", None),
        P("dp", "seq", None),
        P("seq", None),
        P("seq", None, None),
        P("seq", None, None),
    )
    out_specs = (P("dp", "seq", None), P("dp", "seq", None), P(("seq", "dp"), None))
    return jax.shard_map(
        functools.partial(per_device, ranks=mesh.shape["seq"], groups=mesh.shape["dp"]),
        mesh=mesh,
        in_specs=in_specs,
        out_specs=out_specs,
        check_vma=False,
    )
```

```python
import functools

import jax
import jax.numpy as jnp
from jax import lax
from jax.experimental import pallas as pl
from jax.experimental.pallas import tpu as pltpu
from jax.sharding import PartitionSpec as P

WIDTH = 128
ROWS = 16
VMEM_LIMIT = 60 * 1024 * 1024
BACK_LIMIT = 40 * 1024 * 1024
COST = pl.CostEstimate(flops=1024, bytes_accessed=1024, transcendentals=0)
FIRST = 5
EARLY = 3
UNROLL = 8
TOKEN = (8, 128)


def moves_of(ranks):
    far, near = list(range(ranks - 2, ranks)), list(range(2, ranks - 2))
    return [0, far[0]] + near[::2] + [far[1]] + near[1::2] + [1]


def left_forward_kernel(ranks, rank_ref, values_ref, cotangent_ref, left_ref, *refs):
    moves = moves_of(ranks)
    *sends, token_ref = refs[-ranks - 1 :]
    token_ref[...] = jnp.zeros_like(token_ref)
    blocks, order, _ = left_ref.shape
    share = order // ranks
    rank = rank_ref[0]
    for i in range(blocks):
        rows = slice(i * order, (i + 1) * order)
        source = values_ref[0, rows, :]
        gated = source.astype(jnp.float32) * cotangent_ref[0, rows, :].astype(jnp.float32)
        both = jnp.concatenate([source, gated.astype(jnp.bfloat16)], axis=1)
        factor = jnp.concatenate(
            [left_ref[i, pl.ds(pl.multiple_of((rank ^ m) * share, share), share), :] for m in moves],
            axis=0,
        )
        first = jnp.dot(factor, both, preferred_element_type=jnp.float32).astype(jnp.bfloat16)
        for m in range(ranks):
            sends[m][i] = first[m * share : (m + 1) * share]


def right_kernel(ranks, arrived_parts, sent_parts, rank_ref, kernel_ref, right_ref, *refs):
    arrived = refs[: arrived_parts * ranks]
    *sends, term_ref, token_ref, gathered, scattered = refs[-sent_parts * ranks - 4 :]
    token_ref[...] = jnp.zeros_like(token_ref)
    _, rows, lanes = arrived[0].shape
    order = right_ref.shape[1]
    share = order // ranks
    width = lanes // 2
    rank = rank_ref[0]
    halves = [slice(0, width), slice(width, lanes)]

    moves = moves_of(ranks)

    def span(n, part, parts):
        size = share * rows // parts
        start = (rank ^ moves[n]) * (share * rows) + part * size
        return pl.ds(pl.multiple_of(start, size), size)

    for n, block_ref in enumerate(arrived):
        where = span(n % ranks, n // ranks, arrived_parts)
        for half in range(2):
            block = block_ref[:, :, halves[half]].astype(jnp.float32)
            gathered[half, where, :] = block.reshape(where.size, width)

    def step(k, carry):
        both = jnp.concatenate(
            [gathered[half, pl.ds(k, order, stride=rows), :] for half in range(2)], axis=1
        ).astype(jnp.bfloat16)
        factor = right_ref[k]
        result = jnp.dot(factor, both, preferred_element_type=jnp.float32)
        spectrum = result[:, :width].astype(jnp.bfloat16).astype(jnp.float32)
        spectrum_grad = result[:, width:]
        here = pl.ds(pl.multiple_of(k * order, order), order)
        kernel_wide = kernel_ref[here, :].astype(jnp.float32)
        term_ref[here, :] = (spectrum_grad * spectrum).astype(jnp.bfloat16)
        domain = jnp.concatenate(
            [
                (kernel_wide * spectrum).astype(jnp.bfloat16),
                (kernel_wide * spectrum_grad).astype(jnp.bfloat16),
            ],
            axis=1,
        )
        back = lax.dot_general(
            factor, domain, (((0,), (0,)), ((), ())), preferred_element_type=jnp.float32
        )
        for half in range(2):
            scattered[half, pl.ds(k, order, stride=rows), :] = back[:, halves[half]]
        return carry

    def several(g, carry):
        for n in range(UNROLL):
            step(g * UNROLL + n, carry)
        return carry

    lax.fori_loop(0, rows // UNROLL, several, 0)

    for n, block_ref in enumerate(sends):
        where = span(n % ranks, n // ranks, sent_parts)
        for half in range(2):
            block = scattered[half, where, :].astype(jnp.bfloat16)
            block_ref[:, :, halves[half]] = block.reshape(share // sent_parts, rows, width)


def gate_kernel(*refs):
    pass


def left_back_kernel(ranks, terms, rank_ref, values_ref, cotangent_ref, left_ref, *refs):
    moves = moves_of(ranks)
    arrived, reduced = refs[:ranks], refs[ranks : ranks + terms]
    mixed_ref, values_grad_ref, kernel_grad_ref, token_ref = refs[-4:]
    token_ref[...] = jnp.zeros_like(token_ref)
    blocks, order, _ = left_ref.shape
    share = order // ranks
    width = values_ref.shape[2]
    rank = rank_ref[0]
    for i in range(blocks):
        rows = slice(i * order, (i + 1) * order)
        factor = jnp.concatenate(
            [left_ref[i, pl.ds(pl.multiple_of((rank ^ m) * share, share), share), :] for m in moves],
            axis=0,
        )
        back = jnp.concatenate([arrived[m][i] for m in range(ranks)], axis=0)
        result = lax.dot_general(
            factor, back, (((0,), (0,)), ((), ())), preferred_element_type=jnp.float32
        )
        convolved, carried = result[:, :width], result[:, width:]
        source = values_ref[0, rows, :].astype(jnp.float32)
        upstream = cotangent_ref[0, rows, :].astype(jnp.float32)
        mixed_ref[0, rows, :] = (source * convolved).astype(jnp.bfloat16)
        values_grad_ref[0, rows, :] = (upstream * convolved + carried).astype(jnp.bfloat16)
    for n in range(terms):
        lanes = reduced[n].shape[1]
        kernel_grad_ref[:, n * lanes : (n + 1) * lanes] = reduced[n][...].astype(jnp.float32)


def per_device(values, cotangent, kernel, left_factor, right_factor, ranks, groups):
    sequences, row_count, channels = values.shape
    local, order, _ = left_factor.shape
    width = WIDTH
    lanes = 2 * width
    blocks = min(8, local // 2)
    rows = min(ROWS, local)
    chunks = channels // width
    moves = moves_of(ranks)
    rank = lax.axis_index("seq").astype(jnp.int32).reshape(1)
    params = pltpu.CompilerParams(vmem_limit_bytes=VMEM_LIMIT)
    back_params = pltpu.CompilerParams(vmem_limit_bytes=BACK_LIMIT)
    there = {q: 2 if q == 0 else 1 for q in range(chunks)}
    back = {q: 2 if q == chunks - 1 else 1 for q in range(chunks)}

    def buffer(parts):
        return jax.ShapeDtypeStruct((local // parts, local, lanes), jnp.bfloat16)

    def field_spec(q, first=0):
        return pl.BlockSpec((1, blocks * order, width), lambda g, rank: (0, first + g, q))

    def factor_spec(size, first=0):
        return pl.BlockSpec((size, order, order), lambda g, rank: (first + g, 0, 0))

    token = jax.ShapeDtypeStruct(TOKEN, jnp.float32)
    token_spec = pl.BlockSpec(TOKEN, lambda g, rank: (0, 0))

    def unread(after):
        return [pl.BlockSpec(memory_space=pl.ANY)] * len(after)

    def left_forward(q, part, after):
        steps = local // blocks // there[q]
        first = part * steps
        return pl.pallas_call(
            functools.partial(left_forward_kernel, ranks),
            out_shape=[buffer(there[q])] * ranks + [token],
            grid_spec=pltpu.PrefetchScalarGridSpec(
                num_scalar_prefetch=1,
                grid=(steps,),
                in_specs=[field_spec(q, first), field_spec(q, first), factor_spec(blocks, first)]
                + unread(after),
                out_specs=[pl.BlockSpec((blocks, local, lanes), lambda g, rank: (g, 0, 0))] * ranks
                + [token_spec],
            ),
            compiler_params=params,
            cost_estimate=COST,
        )(rank, values, cotangent, left_factor, *after)

    def exchange(sends):
        return [sends[0]] + [
            lax.ppermute(sends[n], "seq", [(r, r ^ moves[n]) for r in range(ranks)])
            for n in range(1, ranks)
        ]

    def right_both(q, arrived, terms, after):
        held = [] if terms is None else [terms]
        ins, outs = there[q], back[q]

        def moved(parts):
            spec = pl.BlockSpec((local // parts, rows, lanes), lambda g, rank: (0, g, 0))
            return [spec] * (parts * ranks)

        return pl.pallas_call(
            functools.partial(right_kernel, ranks, ins, outs),
            out_shape=[buffer(outs)] * (outs * ranks)
            + [jax.ShapeDtypeStruct((row_count, channels), jnp.bfloat16), token],
            grid_spec=pltpu.PrefetchScalarGridSpec(
                num_scalar_prefetch=1,
                grid=(local // rows,),
                in_specs=[
                    pl.BlockSpec((rows * order, width), lambda g, rank: (g, q)),
                    factor_spec(rows),
                ]
                + moved(ins)
                + unread(held)
                + unread(after),
                out_specs=moved(outs)
                + [pl.BlockSpec((rows * order, width), lambda g, rank: (g, q)), token_spec],
                scratch_shapes=[
                    pltpu.VMEM((2, order * rows, width), jnp.float32),
                    pltpu.VMEM((2, order * rows, width), jnp.float32),
                ],
            ),
            input_output_aliases={3 + ins * ranks: outs * ranks} if held else {},
            compiler_params=params,
            cost_estimate=COST,
        )(rank, kernel, right_factor, *arrived, *held, *after)

    def gate(held, after):
        return list(
            pl.pallas_call(
                gate_kernel,
                out_shape=[jax.ShapeDtypeStruct(x.shape, x.dtype) for x in held],
                in_specs=unread(held) + unread(after),
                out_specs=unread(held),
                input_output_aliases={n: n for n in range(len(held))},
                compiler_params=params,
                cost_estimate=COST,
            )(*held, *after)
        )

    def left_back(q, part, arrived, reduced, outputs, after):
        steps = local // blocks // back[q]
        first = part * steps
        shard = row_count // groups
        out_shape = [
            jax.ShapeDtypeStruct(values.shape, jnp.bfloat16),
            jax.ShapeDtypeStruct(values.shape, jnp.bfloat16),
            jax.ShapeDtypeStruct((shard, channels), jnp.float32),
            token,
        ]
        earlier = list(outputs) if outputs else []
        operands = [pltpu.with_memory_space_constraint(x, pltpu.HBM) for x in (values, cotangent, left_factor)]
        reduced = [pltpu.with_memory_space_constraint(x, pltpu.HBM) for x in reduced]
        terms = len(reduced)
        aliases = {4 + ranks + terms + n: n for n in range(len(earlier))}
        grad_spec = pl.BlockSpec((shard // steps, channels), lambda g, rank: (g, 0))
        return pl.pallas_call(
            functools.partial(left_back_kernel, ranks, terms),
            out_shape=out_shape,
            grid_spec=pltpu.PrefetchScalarGridSpec(
                num_scalar_prefetch=1,
                grid=(steps,),
                in_specs=[
                    field_spec(q, first),
                    field_spec(q, first),
                    factor_spec(blocks, first),
                ]
                + [pl.BlockSpec((blocks, local, lanes), lambda g, rank: (g, 0, 0))] * ranks
                + [grad_spec] * terms
                + unread(earlier)
                + unread(after),
                out_specs=[
                    field_spec(q, first),
                    field_spec(q, first),
                    grad_spec if terms else pl.BlockSpec(memory_space=pl.ANY),
                    token_spec,
                ],
            ),
            input_output_aliases=aliases,
            compiler_params=back_params,
            cost_estimate=COST,
        )(rank, *operands, *arrived, *reduced, *earlier, *after)

    received, sent, returned = {}, {}, {}
    left_tokens, right_tokens, back_tokens = [], {}, {}
    terms, outputs = None, []

    parts = {}
    for q in range(chunks):
        parts[q] = []
        for part in range(there[q]):
            *sends, done = left_forward(q, part, left_tokens[-1:])
            left_tokens.append(done)
            parts[q].append(sends)

    def send_left(q):
        received[q] = []
        for sends in parts[q]:
            if q == 1:
                sends[1 + FIRST :] = gate(sends[1 + FIRST :], left_tokens[-1:])
            if q >= 2:
                sends[1 + EARLY :] = gate(sends[1 + EARLY :], [right_tokens[q - 2]])
            received[q] += exchange(sends)

    for q in range(min(2, chunks)):
        send_left(q)
    for q in range(chunks):
        after = [right_tokens[q - 1]] if q else []
        *sent[q], terms, right_tokens[q] = right_both(q, received[q], terms, after)
        if q + 2 < chunks:
            send_left(q + 2)

    def back_step(q):
        last = [reduced] if q == chunks - 1 else []
        for part in range(back[q]):
            arrived = returned[q][part * ranks : (part + 1) * ranks]
            after = [right_tokens[chunks - 1]]
            *outputs[:], back_tokens[q] = left_back(q, part, arrived, last, outputs, after)
            last = []

    for q in range(chunks):
        returned[q] = []
        for part in range(back[q]):
            sends = list(sent[q][part * ranks : (part + 1) * ranks])
            after = []
            if 1 <= q < chunks - 1:
                after.append(right_tokens[chunks - 1])
            if q >= 2:
                after.append(back_tokens[q - 2 + part])
            if q == 0 and chunks > 2:
                sends[1 : 1 + EARLY] = gate(sends[1 : 1 + EARLY], [right_tokens[chunks - 2]])
            if after:
                sends[1:] = gate(sends[1:], after)
            returned[q] += exchange(sends)
            if q >= 1 and part == 0:
                back_step(q - 1)
        if q == 0:
            (terms,) = gate([terms], returned[0][1 : 1 + EARLY])
            reduced = lax.psum_scatter(terms, "dp", scatter_dimension=0, tiled=True)
    back_step(chunks - 1)
    return tuple(outputs)


def solution(mesh):
    in_specs = (
        P("dp", "seq", None),
        P("dp", "seq", None),
        P("seq", None),
        P("seq", None, None),
        P("seq", None, None),
    )
    out_specs = (P("dp", "seq", None), P("dp", "seq", None), P(("seq", "dp"), None))
    return jax.shard_map(
        functools.partial(per_device, ranks=mesh.shape["seq"], groups=mesh.shape["dp"]),
        mesh=mesh,
        in_specs=in_specs,
        out_specs=out_specs,
        check_vma=False,
    )
```

```python
import functools

import jax
import jax.numpy as jnp
from jax import lax
from jax.experimental import pallas as pl
from jax.experimental.pallas import tpu as pltpu
from jax.sharding import PartitionSpec as P

WIDTH = 128
ROWS = 16
VMEM_LIMIT = 60 * 1024 * 1024
BACK_LIMIT = 40 * 1024 * 1024
COST = pl.CostEstimate(flops=1024, bytes_accessed=1024, transcendentals=0)
FIRST = 5
EARLY = 3
UNROLL = 8
TOKEN = (8, 128)


def moves_of(ranks):
    far, near = list(range(ranks - 2, ranks)), list(range(2, ranks - 2))
    return [0, far[0]] + near[::2] + [far[1]] + near[1::2] + [1]


def left_forward_kernel(ranks, rank_ref, values_ref, cotangent_ref, left_ref, *refs):
    moves = moves_of(ranks)
    *sends, token_ref = refs[-ranks - 1 :]
    token_ref[...] = jnp.zeros_like(token_ref)
    blocks, order, _ = left_ref.shape
    share = order // ranks
    rank = rank_ref[0]
    for i in range(blocks):
        rows = slice(i * order, (i + 1) * order)
        source = values_ref[0, rows, :]
        gated = source.astype(jnp.float32) * cotangent_ref[0, rows, :].astype(jnp.float32)
        both = jnp.concatenate([source, gated.astype(jnp.bfloat16)], axis=1)
        factor = jnp.concatenate(
            [left_ref[i, pl.ds(pl.multiple_of((rank ^ m) * share, share), share), :] for m in moves],
            axis=0,
        )
        first = jnp.dot(factor, both, preferred_element_type=jnp.float32).astype(jnp.bfloat16)
        for m in range(ranks):
            sends[m][i] = first[m * share : (m + 1) * share]


def right_kernel(ranks, arrived_parts, sent_parts, rank_ref, kernel_ref, right_ref, *refs):
    arrived = refs[: arrived_parts * ranks]
    *sends, term_ref, token_ref, gathered, scattered = refs[-sent_parts * ranks - 4 :]
    token_ref[...] = jnp.zeros_like(token_ref)
    _, rows, lanes = arrived[0].shape
    order = right_ref.shape[1]
    share = order // ranks
    width = lanes // 2
    rank = rank_ref[0]
    halves = [slice(0, width), slice(width, lanes)]

    moves = moves_of(ranks)

    def span(n, part, parts):
        size = share * rows // parts
        start = (rank ^ moves[n]) * (share * rows) + part * size
        return pl.ds(pl.multiple_of(start, size), size)

    for n, block_ref in enumerate(arrived):
        where = span(n % ranks, n // ranks, arrived_parts)
        for half in range(2):
            block = block_ref[:, :, halves[half]].astype(jnp.float32)
            gathered[half, where, :] = block.reshape(where.size, width)

    def step(k, carry):
        both = jnp.concatenate(
            [gathered[half, pl.ds(k, order, stride=rows), :] for half in range(2)], axis=1
        ).astype(jnp.bfloat16)
        factor = right_ref[k]
        result = jnp.dot(factor, both, preferred_element_type=jnp.float32)
        spectrum = result[:, :width].astype(jnp.bfloat16).astype(jnp.float32)
        spectrum_grad = result[:, width:]
        here = pl.ds(pl.multiple_of(k * order, order), order)
        kernel_wide = kernel_ref[here, :].astype(jnp.float32)
        term_ref[here, :] = (spectrum_grad * spectrum).astype(jnp.bfloat16)
        domain = jnp.concatenate(
            [
                (kernel_wide * spectrum).astype(jnp.bfloat16),
                (kernel_wide * spectrum_grad).astype(jnp.bfloat16),
            ],
            axis=1,
        )
        back = lax.dot_general(
            factor, domain, (((0,), (0,)), ((), ())), preferred_element_type=jnp.float32
        )
        for half in range(2):
            scattered[half, pl.ds(k, order, stride=rows), :] = back[:, halves[half]]
        return carry

    def several(g, carry):
        for n in range(UNROLL):
            step(g * UNROLL + n, carry)
        return carry

    lax.fori_loop(0, rows // UNROLL, several, 0)

    for n, block_ref in enumerate(sends):
        where = span(n % ranks, n // ranks, sent_parts)
        for half in range(2):
            block = scattered[half, where, :].astype(jnp.bfloat16)
            block_ref[:, :, halves[half]] = block.reshape(share // sent_parts, rows, width)


def gate_kernel(*refs):
    pass


def left_back_kernel(ranks, terms, rank_ref, values_ref, cotangent_ref, left_ref, *refs):
    moves = moves_of(ranks)
    arrived, reduced = refs[:ranks], refs[ranks : ranks + terms]
    mixed_ref, values_grad_ref, kernel_grad_ref, token_ref = refs[-4:]
    token_ref[...] = jnp.zeros_like(token_ref)
    blocks, order, _ = left_ref.shape
    share = order // ranks
    width = values_ref.shape[2]
    rank = rank_ref[0]
    for i in range(blocks):
        rows = slice(i * order, (i + 1) * order)
        factor = jnp.concatenate(
            [left_ref[i, pl.ds(pl.multiple_of((rank ^ m) * share, share), share), :] for m in moves],
            axis=0,
        )
        back = jnp.concatenate([arrived[m][i] for m in range(ranks)], axis=0)
        result = lax.dot_general(
            factor, back, (((0,), (0,)), ((), ())), preferred_element_type=jnp.float32
        )
        convolved, carried = result[:, :width], result[:, width:]
        source = values_ref[0, rows, :].astype(jnp.float32)
        upstream = cotangent_ref[0, rows, :].astype(jnp.float32)
        mixed_ref[0, rows, :] = (source * convolved).astype(jnp.bfloat16)
        values_grad_ref[0, rows, :] = (upstream * convolved + carried).astype(jnp.bfloat16)
    for n in range(terms):
        lanes = reduced[n].shape[1]
        kernel_grad_ref[:, n * lanes : (n + 1) * lanes] = reduced[n][...].astype(jnp.float32)


def per_device(values, cotangent, kernel, left_factor, right_factor, ranks, groups):
    sequences, row_count, channels = values.shape
    local, order, _ = left_factor.shape
    width = WIDTH
    lanes = 2 * width
    blocks = min(8, local // 2)
    rows = min(ROWS, local)
    chunks = channels // width
    moves = moves_of(ranks)
    rank = lax.axis_index("seq").astype(jnp.int32).reshape(1)
    params = pltpu.CompilerParams(vmem_limit_bytes=VMEM_LIMIT)
    back_params = pltpu.CompilerParams(vmem_limit_bytes=BACK_LIMIT)
    there = {q: 2 if q == 0 else 1 for q in range(chunks)}
    back = {q: 2 if q == chunks - 1 else 1 for q in range(chunks)}

    def buffer(parts):
        return jax.ShapeDtypeStruct((local // parts, local, lanes), jnp.bfloat16)

    def field_spec(q, first=0):
        return pl.BlockSpec((1, blocks * order, width), lambda g, rank: (0, first + g, q))

    def factor_spec(size, first=0):
        return pl.BlockSpec((size, order, order), lambda g, rank: (first + g, 0, 0))

    token = jax.ShapeDtypeStruct(TOKEN, jnp.float32)
    token_spec = pl.BlockSpec(TOKEN, lambda g, rank: (0, 0))

    def unread(after):
        return [pl.BlockSpec(memory_space=pl.ANY)] * len(after)

    def left_forward(q, part, after):
        steps = local // blocks // there[q]
        first = part * steps
        return pl.pallas_call(
            functools.partial(left_forward_kernel, ranks),
            out_shape=[buffer(there[q])] * ranks + [token],
            grid_spec=pltpu.PrefetchScalarGridSpec(
                num_scalar_prefetch=1,
                grid=(steps,),
                in_specs=[field_spec(q, first), field_spec(q, first), factor_spec(blocks, first)]
                + unread(after),
                out_specs=[pl.BlockSpec((blocks, local, lanes), lambda g, rank: (g, 0, 0))] * ranks
                + [token_spec],
            ),
            compiler_params=params,
            cost_estimate=COST,
        )(rank, values, cotangent, left_factor, *after)

    def exchange(sends):
        return [sends[0]] + [
            lax.ppermute(sends[n], "seq", [(r, r ^ moves[n]) for r in range(ranks)])
            for n in range(1, ranks)
        ]

    def right_both(q, arrived, terms, after):
        held = [] if terms is None else [terms]
        ins, outs = there[q], back[q]

        def moved(parts):
            spec = pl.BlockSpec((local // parts, rows, lanes), lambda g, rank: (0, g, 0))
            return [spec] * (parts * ranks)

        return pl.pallas_call(
            functools.partial(right_kernel, ranks, ins, outs),
            out_shape=[buffer(outs)] * (outs * ranks)
            + [jax.ShapeDtypeStruct((row_count, channels), jnp.bfloat16), token],
            grid_spec=pltpu.PrefetchScalarGridSpec(
                num_scalar_prefetch=1,
                grid=(local // rows,),
                in_specs=[
                    pl.BlockSpec((rows * order, width), lambda g, rank: (g, q)),
                    factor_spec(rows),
                ]
                + moved(ins)
                + unread(held)
                + unread(after),
                out_specs=moved(outs)
                + [pl.BlockSpec((rows * order, width), lambda g, rank: (g, q)), token_spec],
                scratch_shapes=[
                    pltpu.VMEM((2, order * rows, width), jnp.float32),
                    pltpu.VMEM((2, order * rows, width), jnp.float32),
                ],
            ),
            input_output_aliases={3 + ins * ranks: outs * ranks} if held else {},
            compiler_params=params,
            cost_estimate=COST,
        )(rank, kernel, right_factor, *arrived, *held, *after)

    def gate(held, after, grant=params):
        return list(
            pl.pallas_call(
                gate_kernel,
                out_shape=[jax.ShapeDtypeStruct(x.shape, x.dtype) for x in held],
                in_specs=unread(held) + unread(after),
                out_specs=unread(held),
                input_output_aliases={n: n for n in range(len(held))},
                compiler_params=grant,
                cost_estimate=COST,
            )(*[pltpu.with_memory_space_constraint(x, pltpu.HBM) for x in held], *after)
        )

    def left_back(q, part, arrived, reduced, outputs, after):
        steps = local // blocks // back[q]
        first = part * steps
        shard = row_count // groups
        out_shape = [
            jax.ShapeDtypeStruct(values.shape, jnp.bfloat16),
            jax.ShapeDtypeStruct(values.shape, jnp.bfloat16),
            jax.ShapeDtypeStruct((shard, channels), jnp.float32),
            token,
        ]
        earlier = list(outputs) if outputs else []
        operands = [pltpu.with_memory_space_constraint(x, pltpu.HBM) for x in (values, cotangent, left_factor)]
        reduced = [pltpu.with_memory_space_constraint(x, pltpu.HBM) for x in reduced]
        terms = len(reduced)
        aliases = {4 + ranks + terms + n: n for n in range(len(earlier))}
        grad_spec = pl.BlockSpec((shard // steps, channels), lambda g, rank: (g, 0))
        return pl.pallas_call(
            functools.partial(left_back_kernel, ranks, terms),
            out_shape=out_shape,
            grid_spec=pltpu.PrefetchScalarGridSpec(
                num_scalar_prefetch=1,
                grid=(steps,),
                in_specs=[
                    field_spec(q, first),
                    field_spec(q, first),
                    factor_spec(blocks, first),
                ]
                + [pl.BlockSpec((blocks, local, lanes), lambda g, rank: (g, 0, 0))] * ranks
                + [grad_spec] * terms
                + unread(earlier)
                + unread(after),
                out_specs=[
                    field_spec(q, first),
                    field_spec(q, first),
                    grad_spec if terms else pl.BlockSpec(memory_space=pl.ANY),
                    token_spec,
                ],
            ),
            input_output_aliases=aliases,
            compiler_params=back_params,
            cost_estimate=COST,
        )(rank, *operands, *arrived, *reduced, *earlier, *after)

    received, sent, returned = {}, {}, {}
    left_tokens, right_tokens, back_tokens = [], {}, {}
    terms, outputs = None, []

    parts = {}
    for q in range(chunks):
        parts[q] = []
        for part in range(there[q]):
            *sends, done = left_forward(q, part, left_tokens[-1:])
            left_tokens.append(done)
            parts[q].append(sends)

    def send_left(q):
        received[q] = []
        for sends in parts[q]:
            if q == 1:
                sends[1 + FIRST :] = gate(sends[1 + FIRST :], left_tokens[-1:])
            if q >= 2:
                sends[1 + EARLY :] = gate(sends[1 + EARLY :], [right_tokens[q - 2]])
            received[q] += exchange(sends)

    for q in range(min(2, chunks)):
        send_left(q)
    for q in range(chunks):
        after = [right_tokens[q - 1]] if q else []
        *sent[q], terms, right_tokens[q] = right_both(q, received[q], terms, after)
        if q + 2 < chunks:
            send_left(q + 2)

    def back_step(q):
        last = [reduced] if q == chunks - 1 else []
        for part in range(back[q]):
            arrived = returned[q][part * ranks : (part + 1) * ranks]
            after = [right_tokens[chunks - 1]]
            *outputs[:], back_tokens[q] = left_back(q, part, arrived, last, outputs, after)
            last = []

    for q in range(chunks):
        returned[q] = []
        for part in range(back[q]):
            sends = list(sent[q][part * ranks : (part + 1) * ranks])
            after = []
            if 1 <= q < chunks - 1:
                after.append(right_tokens[chunks - 1])
            if q >= 2:
                after.append(back_tokens[q - 2 + part])
            if q == 0 and chunks > 2:
                sends[1 : 1 + EARLY] = gate(sends[1 : 1 + EARLY], [right_tokens[chunks - 2]])
            if after:
                sends[1:] = gate(sends[1:], after)
            returned[q] += exchange(sends)
            if q >= 1 and part == 0:
                back_step(q - 1)
        if q == 0:
            (terms,) = gate([terms], returned[0][1 : 1 + EARLY], back_params)
            reduced = lax.psum_scatter(terms, "dp", scatter_dimension=0, tiled=True)
    back_step(chunks - 1)
    return tuple(outputs)


def solution(mesh):
    in_specs = (
        P("dp", "seq", None),
        P("dp", "seq", None),
        P("seq", None),
        P("seq", None, None),
        P("seq", None, None),
    )
    out_specs = (P("dp", "seq", None), P("dp", "seq", None), P(("seq", "dp"), None))
    return jax.shard_map(
        functools.partial(per_device, ranks=mesh.shape["seq"], groups=mesh.shape["dp"]),
        mesh=mesh,
        in_specs=in_specs,
        out_specs=out_specs,
        check_vma=False,
    )
```
